128 devices in a mesh: grp: 4 (over z), chan: 32 (over x, y, core).
Axes of the slice: x: 4, y: 4, z: 4, core: 2. Of those that a mesh axis runs over, the one named last changes fastest.
Arguments:
- jones_start: float32 [256, 8, 64, 62], P(('grp', 'chan')), may hold values from -0.9 to 1.9
- duals_start: float32 [256, 8, 64, 62], P(('grp', 'chan')), may hold values from -2.5 to 2.5
- consensus_start: float32 [3, 8, 64, 62], replicated, may hold values from -0.6 to 1.6
- visibilities: float32 [256, 8, 1891], P(('grp', 'chan')), may hold values from -6 to 6
- coherencies: bfloat16 [256, 8, 64, 1891], P(('grp', 'chan')), may hold values from -0.59765625 to 0.59765625
- pairs: int32 [2, 1891], replicated, may hold values from 0 to 61, as said below
- counts: int32 [256], P(('grp', 'chan')), may hold values from 1 to 16
Outputs:
- jones: float32 [256, 8, 64, 62], P(('grp', 'chan'))
- duals: float32 [256, 8, 64, 62], P(('grp', 'chan'))
- consensus: float32 [3, 8, 64, 62], replicated
The draws below stay inside these ranges and needn't reach their ends.
Inputs may be any that keep to these rules, and one draw needn't show every extreme that they name: `pairs`: row 0 and row 1 name the two stations of a baseline; every unordered pair of distinct stations appears exactly once, in either order.
All inputs are finite; a program needn't handle non-finite values.
Results may differ from the reference program's by a relative error of at most 0.0003.
Values sent between devices are 32-bit elements; how exact they have to be, the bound alone decides.
A program may use at most 128 MiB of HBM per device.

```python
import jax
import jax.numpy as jnp
import numpy as np
from jax import lax

STATIONS = 62
DIRS = 64
BASE = 1891
COEFFS = 3
CHANNELS = 256
SAMPLES = 16
STEPS = 2
ITERS = 1


def draw_pairs(key, part):
    key = jax.random.fold_in(key, 11)
    first_table, second_table = np.triu_indices(STATIONS, 1)
    order = jax.random.permutation(jax.random.fold_in(key, 1), BASE)
    swapped = jax.random.randint(jax.random.fold_in(key, 2), (BASE,), 0, 2)
    former = jnp.asarray(first_table, jnp.int32)[order]
    latter = jnp.asarray(second_table, jnp.int32)[order]
    lower = jnp.where(swapped == 1, latter, former)
    upper = jnp.where(swapped == 1, former, latter)
    return jnp.stack([lower, upper]).astype(jnp.int32)


def identity_plus(key, shape, spread_value):
    diagonal = jnp.array([1.0, 0.0, 0.0, 0.0, 0.0, 0.0, 1.0, 0.0], jnp.float32)[None, :, None, None]
    noise = spread_value * jax.random.truncated_normal(key, -3.0, 3.0, shape, jnp.float32)
    return (diagonal + noise).astype(jnp.float32)


def draw_jones_start(key, part):
    key = jax.random.fold_in(key, 21)
    return identity_plus(key, (CHANNELS, 8, DIRS, STATIONS), 0.3)


def draw_consensus_start(key, part):
    key = jax.random.fold_in(key, 31)
    return identity_plus(key, (COEFFS, 8, DIRS, STATIONS), 0.2)


def with_ends(entries, stream_key, smallest, largest):
    longest = entries.shape.index(max(entries.shape))
    spots = []
    for shift in (0, 1):
        where = [jax.random.randint(jax.random.fold_in(stream_key, axis), (), 0, length) for axis, length in enumerate(entries.shape)]
        where[longest] = (where[longest] + shift) % entries.shape[longest]
        spots.append(tuple(where))
    return entries.at[spots[0]].set(smallest).at[spots[1]].set(largest)


def level_of(key, dims, cuts, smallest, high):
    factor_of, own = 1.0, jax.random.fold_in(key, 6)
    for dim, parts in cuts:
        draws = jnp.exp(jax.random.uniform(jax.random.fold_in(own, dim), (parts,), jnp.float32, smallest / len(cuts), high / len(cuts)))
        factor_of = factor_of * jnp.repeat(draws, dims[dim] // parts).reshape([-1 if axis == dim else 1 for axis in range(len(dims))])
    return factor_of


def gaussian(key, dims, width, most, shards=(), kind=jnp.bfloat16):
    level = level_of(key, dims, shards, -0.22, 0.18) if shards else 1.0
    entries = jax.random.normal(key, dims, jnp.float32) * width * level
    return jnp.minimum(jnp.maximum(entries, -most), most).astype(kind)


def setup_inputs(seed: int = 0) -> dict:
    arg_keys = jax.random.split(jax.random.key(seed), 8)
    jones_start = draw_jones_start(jax.random.fold_in(arg_keys[7], 71), 0)
    duals_start = gaussian(arg_keys[1], (CHANNELS, 8, DIRS, STATIONS), 0.3, 2.5, ((0, 128),), jnp.float32)
    consensus_start = draw_consensus_start(jax.random.fold_in(arg_keys[7], 71), 0)
    visibilities = gaussian(arg_keys[3], (CHANNELS, 8, BASE), 1.0, 6.0, ((0, 128),), jnp.float32)
    coherencies = gaussian(arg_keys[4], (CHANNELS, 8, DIRS, BASE), 0.1, 0.59765625, ((0, 128),))
    pairs = draw_pairs(jax.random.fold_in(arg_keys[7], 71), 0)
    counts = with_ends(jax.random.randint(arg_keys[6], (CHANNELS,), 1, SAMPLES + 1), jax.random.fold_in(arg_keys[6], 1), 1, SAMPLES).astype(jnp.int32)
    return dict(jones_start=jones_start, duals_start=duals_start, consensus_start=consensus_start, visibilities=visibilities, coherencies=coherencies, pairs=pairs, counts=counts)


ETA_STEP = 0.08
RHO_PENALTY = 1.0
HIGHEST_PRECISION = lax.Precision.HIGHEST


def as_complex(stacked):
    return [(stacked[0], stacked[1]), (stacked[2], stacked[3]), (stacked[4], stacked[5]), (stacked[6], stacked[7])]


def as_stacked(matrix):
    return jnp.stack([component for element in matrix for component in element])


def complex_product(former, latter):
    return (former[0] * latter[0] - former[1] * latter[1], former[0] * latter[1] + former[1] * latter[0])


def complex_sum(former, latter):
    return (former[0] + latter[0], former[1] + latter[1])


def matrix_product(former, latter):
    upper_left = complex_sum(complex_product(former[0], latter[0]), complex_product(former[1], latter[2]))
    upper_right = complex_sum(complex_product(former[0], latter[1]), complex_product(former[1], latter[3]))
    lower_left = complex_sum(complex_product(former[2], latter[0]), complex_product(former[3], latter[2]))
    lower_right = complex_sum(complex_product(former[2], latter[1]), complex_product(former[3], latter[3]))
    return [upper_left, upper_right, lower_left, lower_right]


def conjugate(element):
    return (element[0], -element[1])


def adjoint(matrix):
    return [conjugate(matrix[0]), conjugate(matrix[2]), conjugate(matrix[1]), conjugate(matrix[3])]


def data_gradient(first_jones, second_jones, coherency, observed, weight):
    first_terms = as_complex(first_jones)
    second_terms = as_complex(second_jones)
    source_terms = as_complex(coherency.astype(jnp.float32))
    propagated = matrix_product(first_terms, source_terms)
    predicted = jnp.sum(as_stacked(matrix_product(propagated, adjoint(second_terms))), axis=1)
    residual = as_complex((observed - predicted)[:, None, :])
    conjugated = matrix_product(second_terms, adjoint(source_terms))
    factor = -2.0 * weight
    grad_first = factor * as_stacked(matrix_product(residual, conjugated))
    grad_second = factor * as_stacked(matrix_product(adjoint(residual), propagated))
    return grad_first, grad_second


def bernstein(position):
    return jnp.stack([(1.0 - position) * (1.0 - position), 2.0 * position * (1.0 - position), position * position])


def inverse_three(matrix):
    cross_rows = jnp.stack([jnp.cross(matrix[1], matrix[2]), jnp.cross(matrix[2], matrix[0]), jnp.cross(matrix[0], matrix[1])])
    determinant = jnp.sum(matrix[0] * cross_rows[0])
    return cross_rows.T / determinant


def gram_inverse(channels):
    position = (jnp.arange(channels, dtype=jnp.float32) + 0.5) / channels
    values = bernstein(position)
    return inverse_three(jnp.dot(values, values.T, precision=HIGHEST_PRECISION))


def descend(jones, duals, target, coherency, observed, weight, collect, spread):
    for step_index in range(STEPS):
        first_jones, second_jones = collect(jones)
        grad_first, grad_second = data_gradient(first_jones, second_jones, coherency, observed, weight)
        gradient = spread(grad_first, grad_second) + RHO_PENALTY * (jones - target) + duals
        jones = jones - ETA_STEP * gradient
    return jones


def reference(jones_start, duals_start, consensus_start, visibilities, coherencies, pairs, counts):
    channels = jones_start.shape[0]
    inverse = gram_inverse(channels)
    basis_values = bernstein((jnp.arange(channels, dtype=jnp.float32) + 0.5) / channels)
    weights = counts.astype(jnp.float32) / SAMPLES
    first_station = pairs[0]
    second_station = pairs[1]

    def collect(jones):
        return jones[:, :, first_station], jones[:, :, second_station]

    def spread(grad_first, grad_second):
        blank = jnp.zeros(jones_start.shape[1:], jnp.float32)
        return blank.at[:, :, first_station].add(grad_first).at[:, :, second_station].add(grad_second)

    jones, duals, consensus = jones_start, duals_start, consensus_start
    for round_index in range(ITERS):
        def update(packed):
            local_jones, local_duals, coherency, observed, weight, column = packed
            target = jnp.einsum('i,ikds->kds', column, consensus, precision=HIGHEST_PRECISION)
            return descend(local_jones, local_duals, target, coherency, observed, weight, collect, spread)

        jones = lax.map(update, (jones, duals, coherencies, visibilities, weights, basis_values.T))
        sums = jnp.einsum('ic,ckds->ikds', basis_values, jones + duals / RHO_PENALTY, precision=HIGHEST_PRECISION)
        consensus = jnp.einsum('ij,jkds->ikds', inverse, sums, precision=HIGHEST_PRECISION)
        smooth = jnp.einsum('ic,ikds->ckds', basis_values, consensus, precision=HIGHEST_PRECISION)
        duals = duals + RHO_PENALTY * (jones - smooth)
    return jones, duals, consensus
```

```python
import functools

import jax
import jax.numpy as jnp
import numpy as np
from jax import lax
from jax.experimental import pallas as pl
from jax.experimental.pallas import tpu as pltpu
from jax.sharding import PartitionSpec as P

SAMPLES = 16
STEPS = 2
ETA_STEP = 0.08
RHO_PENALTY = 1.0
GROUP = 128
TILE = 384
HALF = 32
F32 = jnp.float32
BF16 = jnp.bfloat16
HIGHEST_PRECISION = lax.Precision.HIGHEST


def bernstein(position):
    return [
        (1.0 - position) * (1.0 - position),
        2.0 * position * (1.0 - position),
        position * position,
    ]


def gram_inverse(channels):
    position = (np.arange(channels, dtype=np.float64) + 0.5) / channels
    values = np.stack(bernstein(position))
    matrix = values @ values.T
    rows = [np.cross(matrix[1], matrix[2]), np.cross(matrix[2], matrix[0]), np.cross(matrix[0], matrix[1])]
    return np.stack(rows).T / np.sum(matrix[0] * rows[0])


def product(a, b):
    out = []
    for row in range(2):
        for col in range(2):
            lr, li = a[4 * row], a[4 * row + 1]
            mr, mi = a[4 * row + 2], a[4 * row + 3]
            br, bi = b[2 * col], b[2 * col + 1]
            dr, di = b[4 + 2 * col], b[4 + 2 * col + 1]
            out.append((lr * br - li * bi) + (mr * dr - mi * di))
            out.append((lr * bi + li * br) + (mr * di + mi * dr))
    return out


def product_adjoint(a, b):
    out = []
    for row in range(2):
        for col in range(2):
            lr, li = a[4 * row], a[4 * row + 1]
            mr, mi = a[4 * row + 2], a[4 * row + 3]
            br, bi = b[4 * col], b[4 * col + 1]
            dr, di = b[4 * col + 2], b[4 * col + 3]
            out.append((lr * br + li * bi) + (mr * dr + mi * di))
            out.append((li * br - lr * bi) + (mi * dr - mr * di))
    return out


def adjoint_product(a, b):
    out = []
    for row in range(2):
        for col in range(2):
            lr, li = a[2 * row], a[2 * row + 1]
            mr, mi = a[4 + 2 * row], a[4 + 2 * row + 1]
            br, bi = b[2 * col], b[2 * col + 1]
            dr, di = b[4 + 2 * col], b[4 + 2 * col + 1]
            out.append((lr * br + li * bi) + (mr * dr + mi * di))
            out.append((lr * bi - li * br) + (mr * di - mi * dr))
    return out


def split(value):
    high = value.astype(BF16)
    low = (value - high.astype(F32)).astype(BF16)
    return high, low


def descend_kernel(
    channels, blocks, pairs_ref, counts_ref, jones_ref, duals_ref, consensus_ref, vis_ref, coh_ref,
    jones_out, sums_out,
    pairs_pad, vis_pad, coh_tail, gather_hot, spread_hot, jones_cur, jones_split, base, first_all,
    second_all, propagated_all, partial_pred, residual_all, grad_parts,
):
    own, _, dirs, stations = jones_ref.shape
    count = pairs_ref.shape[1]
    tiles = gather_hot.shape[0]
    full = (count // GROUP) * GROUP
    halves = dirs // HALF
    chunks = own * halves
    per_tile = TILE // GROUP
    offset = (lax.axis_index("grp") * blocks + lax.axis_index("chan")) * own

    pairs_pad[...] = jnp.full(pairs_pad.shape, -1, jnp.int32)
    pairs_pad[0:2, 0:count] = pairs_ref[...]
    vis_pad[...] = jnp.zeros(vis_pad.shape, F32)
    vis_pad[:, :, 0:count] = vis_ref[...]
    coh_tail[...] = jnp.zeros(coh_tail.shape, BF16)
    coh_tail[:, :, :, 0 : count - full] = coh_ref[:, :, :, full:count]

    ids = lax.broadcasted_iota(jnp.int32, (GROUP, GROUP), 0)
    for tile in range(tiles):
        for part in range(per_tile):
            lanes = slice(tile * TILE + part * GROUP, tile * TILE + (part + 1) * GROUP)
            for side in range(2):
                row = pairs_pad[side : side + 1, lanes]
                hot = jnp.where(ids == row, 1.0, 0.0).astype(BF16)
                where = side * TILE + part * GROUP
                gather_hot[tile, 0:GROUP, where : where + GROUP] = hot
                gather_hot[tile, GROUP : 2 * GROUP, where : where + GROUP] = hot
                for half in range(2):
                    where = (2 * side + half) * TILE + part * GROUP
                    spread_hot[tile, :, where : where + GROUP] = hot

    jones_cur[...] = jnp.zeros(jones_cur.shape, F32)
    base[...] = jnp.zeros(base.shape, F32)
    basis = []
    for channel in range(own):
        position = ((offset + channel).astype(F32) + 0.5) * (1.0 / channels)
        basis.append(bernstein(position))
        for half in range(halves):
            where = slice(half * HALF, (half + 1) * HALF)
            chunk = channel * halves + half
            target = sum(basis[channel][i] * consensus_ref[i, :, where, :] for i in range(3))
            base[chunk, :, :, 0:stations] = ETA_STEP * (RHO_PENALTY * target - duals_ref[channel, :, where, :])
            jones_cur[chunk, :, :, 0:stations] = jones_ref[channel, :, where, :]

    def divide(chunk):
        value = jones_cur[chunk].reshape(8 * HALF, GROUP)
        high, low = split(value)
        jones_split[chunk, :, 0:GROUP] = high
        jones_split[chunk, :, GROUP : 2 * GROUP] = low

    for chunk in range(chunks):
        divide(chunk)

    def coherency(channel, comp, start, group):
        if group * GROUP < full:
            value = coh_ref[channel, comp, pl.ds(start, 16), group * GROUP : (group + 1) * GROUP]
        else:
            value = coh_tail[channel, comp, pl.ds(start, 16), :]
        return value.astype(F32)

    def predict(chunk, _):
        channel, half = chunk // halves, chunk % halves
        for tile in range(tiles):
            both = jnp.dot(jones_split[chunk], gather_hot[tile], preferred_element_type=F32)
            first_all[tile] = both[:, 0:TILE]
            second_all[chunk, tile] = both[:, TILE : 2 * TILE]
            for part in range(per_tile):
                group = tile * per_tile + part
                lanes = slice(part * GROUP, (part + 1) * GROUP)
                total = None
                for deep in range(HALF // 16):
                    start = pl.multiple_of(half * HALF + deep * 16, 16)
                    rows = [slice(c * HALF + deep * 16, c * HALF + deep * 16 + 16) for c in range(8)]
                    source = [coherency(channel, c, start, group) for c in range(8)]
                    first = [first_all[tile, rows[c], lanes] for c in range(8)]
                    second = [second_all[chunk, tile, rows[c], lanes] for c in range(8)]
                    propagated = product(first, source)
                    for c in range(8):
                        propagated_all[chunk, tile, rows[c], lanes] = propagated[c]
                    model = product_adjoint(propagated, second)
                    model = [m[0:8] + m[8:16] for m in model]
                    total = model if total is None else [t + m for t, m in zip(total, model)]
                for c in range(8):
                    partial_pred[chunk, c, :, group * GROUP : (group + 1) * GROUP] = total[c]
        return 0

    def correct(chunk, _):
        channel, half = chunk // halves, chunk % halves
        total = None
        for tile in range(tiles):
            for part in range(per_tile):
                group = tile * per_tile + part
                lanes = slice(part * GROUP, (part + 1) * GROUP)
                residual = [
                    jnp.broadcast_to(
                        residual_all[channel, c : c + 1, group * GROUP : (group + 1) * GROUP], (16, GROUP)
                    )
                    for c in range(8)
                ]
                for deep in range(HALF // 16):
                    start = pl.multiple_of(half * HALF + deep * 16, 16)
                    rows = [slice(c * HALF + deep * 16, c * HALF + deep * 16 + 16) for c in range(8)]
                    source = [coherency(channel, c, start, group) for c in range(8)]
                    second = [second_all[chunk, tile, rows[c], lanes] for c in range(8)]
                    conjugated = product_adjoint(second, source)
                    grad_first = product(residual, conjugated)
                    for c in range(8):
                        high, low = split(grad_first[c])
                        grad_parts[tile, rows[c], part * GROUP : (part + 1) * GROUP] = high
                        grad_parts[tile, rows[c], TILE + part * GROUP : TILE + (part + 1) * GROUP] = low
                    propagated = [propagated_all[chunk, tile, rows[c], lanes] for c in range(8)]
                    grad_second = adjoint_product(residual, propagated)
                    for c in range(8):
                        high, low = split(grad_second[c])
                        grad_parts[tile, rows[c], 2 * TILE + part * GROUP : 2 * TILE + (part + 1) * GROUP] = high
                        grad_parts[tile, rows[c], 3 * TILE + part * GROUP : 3 * TILE + (part + 1) * GROUP] = low
            piece = lax.dot_general(
                grad_parts[tile], spread_hot[tile], (((1,), (1,)), ((), ())), preferred_element_type=F32
            )
            total = piece if total is None else total + piece
        update = total.reshape(8, HALF, GROUP)
        jones_cur[chunk] = (1.0 - ETA_STEP * RHO_PENALTY) * jones_cur[chunk] + base[chunk] + update
        divide(chunk)
        return 0

    for _ in range(STEPS):
        lax.fori_loop(0, chunks, predict, 0)
        for channel in range(own):
            factor = counts_ref[channel].astype(F32) * (2.0 * ETA_STEP / SAMPLES)
            for group in range(tiles * per_tile):
                lanes = slice(group * GROUP, (group + 1) * GROUP)
                total = sum(partial_pred[channel * halves + half, :, :, lanes] for half in range(halves))
                residual_all[channel, :, lanes] = (vis_pad[channel, :, lanes] - jnp.sum(total, axis=1)) * factor
        lax.fori_loop(0, chunks, correct, 0)

    for half in range(halves):
        where = slice(half * HALF, (half + 1) * HALF)
        jones = [jones_cur[channel * halves + half][:, :, 0:stations] for channel in range(own)]
        joined = [jones[channel] + duals_ref[channel, :, where, :] * (1.0 / RHO_PENALTY) for channel in range(own)]
        for channel in range(own):
            jones_out[channel, :, where, :] = jones[channel]
        for i in range(3):
            sums_out[i, :, where, :] = sum(basis[channel][i] * joined[channel] for channel in range(own))


def descend(channels, blocks, pairs, counts, jones, duals, consensus, visibilities, coherencies):
    own, _, dirs, stations = jones.shape
    count = pairs.shape[1]
    tiles = -(-count // TILE)
    lanes = tiles * TILE
    chunks = own * (dirs // HALF)
    rows = 8 * HALF
    vmem = pl.BlockSpec(memory_space=pltpu.VMEM)
    smem = pl.BlockSpec(memory_space=pltpu.SMEM)
    return pl.pallas_call(
        functools.partial(descend_kernel, channels, blocks),
        out_shape=(
            jax.ShapeDtypeStruct(jones.shape, F32),
            jax.ShapeDtypeStruct(consensus.shape, F32),
        ),
        in_specs=[vmem, smem, vmem, vmem, vmem, vmem, vmem],
        out_specs=(vmem, vmem),
        scratch_shapes=[
            pltpu.VMEM((8, lanes), jnp.int32),
            pltpu.VMEM((own, 8, lanes), F32),
            pltpu.VMEM((own, 8, dirs, GROUP), BF16),
            pltpu.VMEM((tiles, 2 * GROUP, 2 * TILE), BF16),
            pltpu.VMEM((tiles, GROUP, 4 * TILE), BF16),
            pltpu.VMEM((chunks, 8, HALF, GROUP), F32),
            pltpu.VMEM((chunks, rows, 2 * GROUP), BF16),
            pltpu.VMEM((chunks, 8, HALF, GROUP), F32),
            pltpu.VMEM((tiles, rows, TILE), F32),
            pltpu.VMEM((chunks, tiles, rows, TILE), F32),
            pltpu.VMEM((chunks, tiles, rows, TILE), F32),
            pltpu.VMEM((chunks, 8, 8, lanes), F32),
            pltpu.VMEM((own, 8, lanes), F32),
            pltpu.VMEM((tiles, rows, 4 * TILE), BF16),
        ],
        compiler_params=pltpu.CompilerParams(vmem_limit_bytes=56 * 2**20),
        name="descend",
    )(pairs, counts, jones, duals, consensus, visibilities, coherencies)


def shards(jones_start, duals_start, consensus_start, visibilities, coherencies, pairs, counts):
    own = jones_start.shape[0]
    blocks = lax.axis_size("chan")
    channels = own * lax.axis_size("grp") * blocks
    offset = (lax.axis_index("grp") * blocks + lax.axis_index("chan")) * own
    jones, local_sums = descend(
        channels, blocks, pairs, counts, jones_start, duals_start, consensus_start, visibilities, coherencies
    )
    sums = lax.psum(local_sums, ("grp", "chan"))
    inverse = gram_inverse(channels).astype(np.float32)
    consensus = jnp.stack([sum(inverse[i, j] * sums[j] for j in range(3)) for i in range(3)])
    duals = []
    for channel in range(own):
        position = ((offset + channel).astype(F32) + 0.5) * (1.0 / channels)
        basis = bernstein(position)
        smooth = sum(basis[i] * consensus[i] for i in range(3))
        duals.append(duals_start[channel] + RHO_PENALTY * (jones[channel] - smooth))
    return (jones, jnp.stack(duals), consensus)


def solution(mesh):
    in_specs = (
        P(("grp", "chan"), None, None, None),
        P(("grp", "chan"), None, None, None),
        P(),
        P(("grp", "chan"), None, None),
        P(("grp", "chan"), None, None, None),
        P(),
        P(("grp", "chan")),
    )
    out_specs = (P(("grp", "chan"), None, None, None), P(("grp", "chan"), None, None, None), P())
    return jax.shard_map(shards, mesh=mesh, in_specs=in_specs, out_specs=out_specs, check_vma=False)
```

```python
import functools

import jax
import jax.numpy as jnp
import numpy as np
from jax import lax
from jax.experimental import pallas as pl
from jax.experimental.pallas import tpu as pltpu
from jax.sharding import PartitionSpec as P

SAMPLES = 16
STEPS = 2
ETA_STEP = 0.08
RHO_PENALTY = 1.0
GROUP = 128
F32 = jnp.float32
BF16 = jnp.bfloat16
MESH = pl.DeviceIdType.MESH
SIDE = 4


def bernstein(position):
    return [
        (1.0 - position) * (1.0 - position),
        2.0 * position * (1.0 - position),
        position * position,
    ]


def gram_inverse(channels):
    position = (np.arange(channels, dtype=np.float64) + 0.5) / channels
    values = np.stack(bernstein(position))
    matrix = values @ values.T
    rows = [np.cross(matrix[1], matrix[2]), np.cross(matrix[2], matrix[0]), np.cross(matrix[0], matrix[1])]
    return np.stack(rows).T / np.sum(matrix[0] * rows[0])


def product_terms(a, b):
    for row in range(2):
        for col in range(2):
            lr, li = a[4 * row], a[4 * row + 1]
            mr, mi = a[4 * row + 2], a[4 * row + 3]
            br, bi = b[2 * col], b[2 * col + 1]
            dr, di = b[4 + 2 * col], b[4 + 2 * col + 1]
            yield ((lr * br - li * bi) + (mr * dr - mi * di))
            yield ((lr * bi + li * br) + (mr * di + mi * dr))


def product(a, b):
    return list(product_terms(a, b))


def product_adjoint_terms(a, b):
    for row in range(2):
        for col in range(2):
            lr, li = a[4 * row], a[4 * row + 1]
            mr, mi = a[4 * row + 2], a[4 * row + 3]
            br, bi = b[4 * col], b[4 * col + 1]
            dr, di = b[4 * col + 2], b[4 * col + 3]
            yield ((lr * br + li * bi) + (mr * dr + mi * di))
            yield ((li * br - lr * bi) + (mi * dr - mr * di))


def product_adjoint(a, b):
    return list(product_adjoint_terms(a, b))


def adjoint_product_terms(a, b):
    for row in range(2):
        for col in range(2):
            lr, li = a[2 * row], a[2 * row + 1]
            mr, mi = a[4 + 2 * row], a[4 + 2 * row + 1]
            br, bi = b[2 * col], b[2 * col + 1]
            dr, di = b[4 + 2 * col], b[4 + 2 * col + 1]
            yield ((lr * br + li * bi) + (mr * dr + mi * di))
            yield ((lr * bi - li * br) + (mr * di - mi * dr))


def adjoint_product(a, b):
    return list(adjoint_product_terms(a, b))


def split(value):
    high = value.astype(BF16)
    low = (value - high.astype(F32)).astype(BF16)
    return high, low


def descend_kernel(
    channels, blocks, pairs_ref, counts_ref, jones_ref, duals_ref, consensus_ref, vis_ref, coh_ref,
    jones_out, sums_out,
    pairs_pad, vis_pad, coh_tail, gather_hot, spread_hot, jones_cur, jones_split, base, turned, both_now,
    propagated_now, grad_parts, update_now,
):
    own, stations, _, dirs = jones_ref.shape
    count = pairs_ref.shape[1]
    groups = gather_hot.shape[0]
    full = count // GROUP
    rows = 8 * dirs
    offset = (lax.axis_index("grp") * blocks + lax.axis_index("chan")) * own

    pairs_pad[...] = jnp.full(pairs_pad.shape, -1, jnp.int32)
    pairs_pad[0:2, 0:count] = pairs_ref[...]
    vis_pad[...] = jnp.zeros(vis_pad.shape, F32)
    vis_pad[:, :, 0:count] = vis_ref[...]
    coh_tail[...] = jnp.zeros(coh_tail.shape, BF16)
    coh_tail[:, :, :, 0 : count - full * GROUP] = coh_ref[:, :, :, full * GROUP : count]

    ids = lax.broadcasted_iota(jnp.int32, (GROUP, GROUP), 0)
    for group in range(groups):
        for side in range(2):
            row = pairs_pad[side : side + 1, group * GROUP : (group + 1) * GROUP]
            hot = jnp.where(ids == row, 1.0, 0.0).astype(BF16)
            for part in range(2):
                gather_hot[group, part * GROUP : (part + 1) * GROUP, side * GROUP : (side + 1) * GROUP] = hot
                where = (2 * side + part) * GROUP
                spread_hot[group, :, where : where + GROUP] = hot

    basis = []
    for channel in range(own):
        position = ((offset + channel).astype(F32) + 0.5) * (1.0 / channels)
        basis.append(bernstein(position))
        target = sum(basis[channel][i] * consensus_ref[i] for i in range(3))
        turned[...] = ETA_STEP * (RHO_PENALTY * target - duals_ref[channel])
        base[channel] = jnp.zeros(base.shape[1:], F32)
        jones_cur[channel] = jnp.zeros(jones_cur.shape[1:], F32)
        for c in range(8):
            base[channel, c, :, 0:stations] = turned[:, c, :].T
            jones_cur[channel, c, :, 0:stations] = jones_ref[channel, :, c, :].T

    def divide(channel):
        high, low = split(jones_cur[channel].reshape(rows, GROUP))
        jones_split[channel, :, 0:GROUP] = high
        jones_split[channel, :, GROUP : 2 * GROUP] = low

    for channel in range(own):
        divide(channel)

    def coherency(channel, group, comp, first):
        if isinstance(group, int) and group == full:
            return coh_tail[channel, comp, first : first + 16, :].astype(F32)
        lanes = pl.ds(pl.multiple_of(group * GROUP, GROUP), GROUP)
        return coh_ref[channel, comp, first : first + 16, lanes].astype(F32)

    def gather(channel, group):
        both_now[channel][...] = jnp.dot(jones_split[channel], gather_hot[group], preferred_element_type=F32)

    def scatter_part(channel, group, side):
        lanes = slice(2 * side * GROUP, 2 * (side + 1) * GROUP)
        update_now[channel][...] += lax.dot_general(
            grad_parts[channel][:, lanes], spread_hot[group, :, lanes], (((1,), (1,)), ((), ())),
            preferred_element_type=F32,
        )

    def scatter(channel, group):
        for side in range(2):
            scatter_part(channel, group, side)

    def visit(channel, group, factor, between=(None, None, None)):
        both, propagated_ref, parts = both_now[channel], propagated_now[channel], grad_parts[channel]
        total = None
        for first_row in range(0, dirs, 16):
            wide = [coherency(channel, group, c, first_row) for c in range(8)]
            for upper in range(2):
                at = [slice(c * dirs + first_row + 8 * upper, c * dirs + first_row + 8 * upper + 8) for c in range(8)]
                source = [w[8 * upper : 8 * upper + 8] for w in wide]
                first = [both[at[c], 0:GROUP] for c in range(8)]
                propagated = product(first, source)
                for c in range(8):
                    propagated_ref[at[c], :] = propagated[c]
                second = [both[at[c], GROUP : 2 * GROUP] for c in range(8)]
                model = product_adjoint(propagated, second)
                total = model if total is None else [t + m for t, m in zip(total, model)]
        if between[0]:
            between[0]()
        lanes = pl.ds(pl.multiple_of(group * GROUP, GROUP), GROUP)
        residual = []
        for c in range(8):
            observed = vis_pad[channel, c : c + 1, lanes]
            value = (observed - jnp.sum(total[c], axis=0, keepdims=True)) * factor
            residual.append(jnp.broadcast_to(value, (16, GROUP)))
        place = [slice(n * GROUP, (n + 1) * GROUP) for n in range(4)]
        for first_row in range(0, dirs, 16):
            at = [slice(c * dirs + first_row, c * dirs + first_row + 16) for c in range(8)]
            source = [coherency(channel, group, c, first_row) for c in range(8)]
            second = [both[at[c], GROUP : 2 * GROUP] for c in range(8)]
            conjugated = product_adjoint(second, source)
            for c, value in enumerate(product_terms(residual, conjugated)):
                parts[at[c], place[0]], parts[at[c], place[1]] = split(value)
            propagated = [propagated_ref[at[c], :] for c in range(8)]
            for c, value in enumerate(adjoint_product_terms(residual, propagated)):
                parts[at[c], place[2]], parts[at[c], place[3]] = split(value)
            if between[1] and first_row == dirs // 2 - 16:
                between[1]()
        if between[2]:
            between[2]()

    factors = [counts_ref[channel].astype(F32) * (2.0 * ETA_STEP / SAMPLES) for channel in range(own)]

    def step(_, carry):
        for channel in range(own):
            update_now[channel][...] = jnp.zeros((rows, GROUP), F32)
        grad_parts[1][...] = jnp.zeros(grad_parts[1].shape, BF16)
        gather(0, 0)

        def sweep(group, carry):
            before = jnp.maximum(group - 1, 0)
            visit(0, group, factors[0], [
                lambda: gather(1, group), lambda: scatter_part(1, before, 0), lambda: scatter_part(1, before, 1)
            ])
            visit(1, group, factors[1], [
                lambda: scatter_part(0, group, 0), lambda: scatter_part(0, group, 1), lambda: gather(0, group + 1)
            ])
            return carry

        lax.fori_loop(0, groups - 1, sweep, 0)
        last = groups - 1
        visit(0, last, factors[0])
        gather(1, last)
        scatter(1, last - 1)
        visit(1, last, factors[1])
        scatter(0, last)
        scatter(1, last)
        for channel in range(own):
            update = update_now[channel][...].reshape(8, dirs, GROUP)
            jones_cur[channel] = (1.0 - ETA_STEP * RHO_PENALTY) * jones_cur[channel] + base[channel] + update
            divide(channel)
        return carry

    lax.fori_loop(0, STEPS, step, 0)

    for channel in range(own):
        for c in range(8):
            jones_out[channel, :, c, :] = jones_cur[channel, c].T[0:stations]
    near = stations // 2
    joined = [jones_out[channel] + duals_ref[channel] * (1.0 / RHO_PENALTY) for channel in range(own)]
    for i in range(3):
        value = sum(basis[channel][i] * joined[channel] for channel in range(own))
        sums_out[0:near, i] = jnp.concatenate([value[0:near], value[near : 2 * near]], axis=2)
        sums_out[near, i] = jnp.zeros((8, GROUP), F32)


def descend(channels, blocks, pairs, counts, jones, duals, consensus, visibilities, coherencies):
    own, stations, _, dirs = jones.shape
    count = pairs.shape[1]
    groups = -(-count // GROUP)
    lanes = groups * GROUP
    rows = 8 * dirs
    vmem = pl.BlockSpec(memory_space=pltpu.VMEM)
    smem = pl.BlockSpec(memory_space=pltpu.SMEM)
    return pl.pallas_call(
        functools.partial(descend_kernel, channels, blocks),
        out_shape=(
            jax.ShapeDtypeStruct(jones.shape, F32),
            jax.ShapeDtypeStruct((stations // 2 + 1, 3, 8, GROUP), F32),
        ),
        in_specs=[vmem, smem, vmem, vmem, vmem, vmem, vmem],
        out_specs=(vmem, vmem),
        scratch_shapes=[
            pltpu.VMEM((8, lanes), jnp.int32),
            pltpu.VMEM((own, 8, lanes), F32),
            pltpu.VMEM((own, 8, dirs, GROUP), BF16),
            pltpu.VMEM((groups, 2 * GROUP, 2 * GROUP), BF16),
            pltpu.VMEM((groups, GROUP, 4 * GROUP), BF16),
            pltpu.VMEM((own, 8, dirs, GROUP), F32),
            pltpu.VMEM((own, rows, 2 * GROUP), BF16),
            pltpu.VMEM((own, 8, dirs, GROUP), F32),
            pltpu.VMEM((stations, 8, dirs), F32),
            [pltpu.VMEM((rows, 2 * GROUP), F32)] * own,
            [pltpu.VMEM((rows, GROUP), F32)] * own,
            [pltpu.VMEM((rows, 4 * GROUP), BF16)] * own,
            [pltpu.VMEM((rows, GROUP), F32)] * own,
        ],
        compiler_params=pltpu.CompilerParams(vmem_limit_bytes=56 * 2**20),
        name="descend",
    )(pairs, counts, jones, duals, consensus, visibilities, coherencies)


def agree_kernel(
    channels, blocks, inverse, s_ref, jones_ref, duals_ref, consensus_out, duals_out,
    recv_core, mid, recv_plane, recv_col, full, s1, r1, s2, r2, s3, r3, s4, r4, s5, r5,
):
    z = lax.axis_index("grp"); chan = lax.axis_index("chan")
    core = chan % 2; u = chan // 2; x = u // SIDE; y = u % SIDE
    other = 1 - core
    def peer(dx, dy):
        return ((x + dx) % SIDE) * SIDE + (y + dy) % SIDE
    steps = sorted([(dx, dy) for dx in range(SIDE) for dy in range(SIDE) if dx or dy], key=lambda s: -(min(s[0],4-s[0])+min(s[1],4-s[1])))
    def back(dx, dy):
        return ((x - dx + SIDE) % SIDE) * SIDE + (y - dy + SIDE) % SIDE
    def dev(uu, cc): return {"grp": z, "chan": uu * 2 + cc}
    barrier = pltpu.get_barrier_semaphore()
    pl.semaphore_signal(barrier, inc=1, device_id=dev(u, other), device_id_type=MESH)
    for dx, dy in steps:
        pl.semaphore_signal(barrier, inc=1, device_id=dev(peer(dx, dy), core), device_id_type=MESH)
    for dz in range(1, SIDE):
        pl.semaphore_signal(barrier, inc=1, device_id={"grp": (z + dz) % SIDE, "chan": chan}, device_id_type=MESH)
    pl.semaphore_wait(barrier, 1 + len(steps) + SIDE - 1)
    order = steps + [(0, 0)]
    def rc(src, dst, ss, rs, d):
        return pltpu.make_async_remote_copy(src_ref=src, dst_ref=dst, send_sem=ss, recv_sem=rs, device_id=d, device_id_type=MESH)
    c1 = []
    for n, (dx, dy) in enumerate(order):
        c = rc(s_ref.at[other * 16 + peer(dx, dy)], recv_core.at[n], s1.at[n], r1.at[n], dev(u, other))
        c.start(); c1.append(c)
    c2 = []
    for n, (dx, dy) in enumerate(order):
        c1[n].wait_recv()
        mid[n] = s_ref[core * 16 + peer(dx, dy)] + recv_core[n]
        if n < 15:
            c = rc(mid.at[n], recv_plane.at[n], s2.at[n], r2.at[n], dev(peer(dx, dy), core))
            c.start(); c2.append(c)
    total = mid[15]
    for n in range(15):
        c2[n].wait_recv()
        total = total + recv_plane[n]
    recv_col[z] = total
    c3 = []
    for dz in range(1, SIDE):
        c = rc(recv_col.at[z], recv_col.at[z], s3.at[dz], r3.at[dz], {"grp": (z + dz) % SIDE, "chan": chan})
        c.start(); c3.append(c)
    for c in c3: c.wait_recv()
    total = recv_col[0] + recv_col[1] + recv_col[2] + recv_col[3]
    mine = core * 16 + u
    for i in range(3):
        full[mine, i] = sum(inverse[i][j] * total[j] for j in range(3))
    c4 = []
    for n, (dx, dy) in enumerate(steps):
        c = rc(full.at[mine], full.at[mine], s4.at[n], r4.at[n], dev(peer(dx, dy), core))
        c.start(); c4.append(c)
    c5 = []
    c = rc(full.at[mine], full.at[mine], s5.at[15], r5.at[15], dev(u, other))
    c.start(); c5.append(c)
    for n, (dx, dy) in reversed(list(enumerate(steps))):
        c4[n].wait_recv()
        unit = core * 16 + back(dx, dy)
        c = rc(full.at[unit], full.at[unit], s5.at[n], r5.at[n], dev(u, other))
        c.start(); c5.append(c)
    for c in c5: c.wait_recv()
    for c in c1 + c2 + c3 + c4 + c5: c.wait_send()
    own, stations, _, dirs = jones_ref.shape
    near = stations // 2
    for i in range(3):
        consensus_out[i, 0:near] = full[0:near, i, :, 0:dirs]
        consensus_out[i, near : 2 * near] = full[0:near, i, :, dirs : 2 * dirs]
    offset = (z * blocks + chan) * own
    for channel in range(own):
        basis = bernstein(((offset + channel).astype(F32) + 0.5) * (1.0 / channels))
        smooth = sum(basis[i] * consensus_out[i] for i in range(3))
        duals_out[channel] = duals_ref[channel] + RHO_PENALTY * (jones_ref[channel] - smooth)


def agree(channels, blocks, sums, jones, duals):
    inverse = [[float(v) for v in row] for row in gram_inverse(channels).astype(np.float32)]
    vmem = pl.BlockSpec(memory_space=pltpu.VMEM)
    unit = sums.shape[1:]
    dma = pltpu.SemaphoreType.DMA
    return pl.pallas_call(
        functools.partial(agree_kernel, channels, blocks, inverse),
        out_shape=(jax.ShapeDtypeStruct((3,) + jones.shape[1:], F32), jax.ShapeDtypeStruct(duals.shape, F32)),
        in_specs=[vmem] * 3,
        out_specs=(vmem, vmem),
        scratch_shapes=[pltpu.VMEM((SIDE * SIDE,) + unit, F32)] * 3
        + [pltpu.VMEM((SIDE,) + unit, F32), pltpu.VMEM((2 * SIDE * SIDE,) + unit, F32)]
        + [dma((SIDE * SIDE,))] * 4
        + [dma((SIDE,))] * 2
        + [dma((SIDE * SIDE,))] * 4,
        compiler_params=pltpu.CompilerParams(
            collective_id=0, has_side_effects=True, vmem_limit_bytes=32 * 2**20
        ),
        name="agree",
    )(sums, jones, duals)


def shards(jones_start, duals_start, consensus_start, visibilities, coherencies, pairs, counts):
    blocks = lax.axis_size("chan")
    channels = jones_start.shape[0] * lax.axis_size("grp") * blocks
    jones, duals, consensus = (jnp.transpose(a, (0, 3, 1, 2)) for a in (jones_start, duals_start, consensus_start))
    jones, sums = descend(channels, blocks, pairs, counts, jones, duals, consensus, visibilities, coherencies)
    consensus, duals = agree(channels, blocks, sums, jones, duals)
    return tuple(jnp.transpose(a, (0, 2, 3, 1)) for a in (jones, duals, consensus))


def solution(mesh):
    in_specs = (
        P(("grp", "chan"), None, None, None),
        P(("grp", "chan"), None, None, None),
        P(),
        P(("grp", "chan"), None, None),
        P(("grp", "chan"), None, None, None),
        P(),
        P(("grp", "chan")),
    )
    out_specs = (P(("grp", "chan"), None, None, None), P(("grp", "chan"), None, None, None), P())
    return jax.shard_map(shards, mesh=mesh, in_specs=in_specs, out_specs=out_specs, check_vma=False)
```

```python
import functools

import jax
import jax.numpy as jnp
import numpy as np
from jax import lax
from jax.experimental import pallas as pl
from jax.experimental.pallas import tpu as pltpu
from jax.sharding import PartitionSpec as P

SAMPLES = 16
STEPS = 2
ETA_STEP = 0.08
RHO_PENALTY = 1.0
GROUP = 128
F32 = jnp.float32
BF16 = jnp.bfloat16
MESH = pl.DeviceIdType.MESH
SIDE = 4


def bernstein(position):
    return [
        (1.0 - position) * (1.0 - position),
        2.0 * position * (1.0 - position),
        position * position,
    ]


def gram_inverse(channels):
    position = (np.arange(channels, dtype=np.float64) + 0.5) / channels
    values = np.stack(bernstein(position))
    matrix = values @ values.T
    rows = [np.cross(matrix[1], matrix[2]), np.cross(matrix[2], matrix[0]), np.cross(matrix[0], matrix[1])]
    return np.stack(rows).T / np.sum(matrix[0] * rows[0])


def product_terms(a, b):
    for row in range(2):
        for col in range(2):
            lr, li = a[4 * row], a[4 * row + 1]
            mr, mi = a[4 * row + 2], a[4 * row + 3]
            br, bi = b[2 * col], b[2 * col + 1]
            dr, di = b[4 + 2 * col], b[4 + 2 * col + 1]
            yield ((lr * br - li * bi) + (mr * dr - mi * di))
            yield ((lr * bi + li * br) + (mr * di + mi * dr))


def product(a, b):
    return list(product_terms(a, b))


def product_adjoint_terms(a, b):
    for row in range(2):
        for col in range(2):
            lr, li = a[4 * row], a[4 * row + 1]
            mr, mi = a[4 * row + 2], a[4 * row + 3]
            br, bi = b[4 * col], b[4 * col + 1]
            dr, di = b[4 * col + 2], b[4 * col + 3]
            yield ((lr * br + li * bi) + (mr * dr + mi * di))
            yield ((li * br - lr * bi) + (mi * dr - mr * di))


def product_adjoint(a, b):
    return list(product_adjoint_terms(a, b))


def adjoint_product_terms(a, b):
    for row in range(2):
        for col in range(2):
            lr, li = a[2 * row], a[2 * row + 1]
            mr, mi = a[4 + 2 * row], a[4 + 2 * row + 1]
            br, bi = b[2 * col], b[2 * col + 1]
            dr, di = b[4 + 2 * col], b[4 + 2 * col + 1]
            yield ((lr * br + li * bi) + (mr * dr + mi * di))
            yield ((lr * bi - li * br) + (mr * di - mi * dr))


def adjoint_product(a, b):
    return list(adjoint_product_terms(a, b))


def split(value):
    high = value.astype(BF16)
    low = (value - high.astype(F32)).astype(BF16)
    return high, low


def greet(wait):
    barrier = pltpu.get_barrier_semaphore()
    z, chan = lax.axis_index("grp"), lax.axis_index("chan")
    core, u = chan % 2, chan // 2
    if wait:
        pl.semaphore_wait(barrier, 1 + SIDE * SIDE - 1 + SIDE - 1)
        return
    pl.semaphore_signal(barrier, inc=1, device_id={"grp": z, "chan": u * 2 + 1 - core}, device_id_type=MESH)
    for dx in range(SIDE):
        for dy in range(SIDE):
            if dx or dy:
                there = ((u // SIDE + dx) % SIDE) * SIDE + (u % SIDE + dy) % SIDE
                pl.semaphore_signal(
                    barrier, inc=1, device_id={"grp": z, "chan": there * 2 + core}, device_id_type=MESH
                )
    for dz in range(1, SIDE):
        pl.semaphore_signal(barrier, inc=1, device_id={"grp": (z + dz) % SIDE, "chan": chan}, device_id_type=MESH)


def descend_kernel(
    channels, blocks, inverse, pairs_ref, counts_ref, jones_ref, duals_ref, consensus_ref, vis_ref, coh_ref,
    jones_out, duals_out, consensus_out, sums_out,
    pairs_pad, vis_pad, coh_tail, spread_hot, jones_cur, base, turned, both_now,
    propagated_now, grad_parts, update_now, *links,
):
    own, stations, _, dirs = jones_ref.shape
    count = pairs_ref.shape[1]
    groups = spread_hot.shape[0]
    full = count // GROUP
    rows = 8 * dirs
    offset = (lax.axis_index("grp") * blocks + lax.axis_index("chan")) * own

    greet(False)

    pairs_pad[...] = jnp.full(pairs_pad.shape, -1, jnp.int32)
    pairs_pad[0:2, 0:count] = pairs_ref[...]
    vis_pad[...] = jnp.zeros(vis_pad.shape, F32)
    vis_pad[:, :, 0:count] = vis_ref[...]
    coh_tail[...] = jnp.zeros(coh_tail.shape, BF16)
    coh_tail[:, :, :, 0 : count - full * GROUP] = coh_ref[:, :, :, full * GROUP : count]

    ids = lax.broadcasted_iota(jnp.int32, (GROUP, GROUP), 0)
    for group in range(groups):
        for side in range(2):
            row = pairs_pad[side : side + 1, group * GROUP : (group + 1) * GROUP]
            hot = jnp.where(ids == row, 1.0, 0.0).astype(BF16)
            for part in range(2):
                where = (2 * side + part) * GROUP
                spread_hot[group, :, where : where + GROUP] = hot

    basis = []
    for channel in range(own):
        position = ((offset + channel).astype(F32) + 0.5) * (1.0 / channels)
        basis.append(bernstein(position))
        target = sum(basis[channel][i] * consensus_ref[i] for i in range(3))
        turned[...] = ETA_STEP * (RHO_PENALTY * target - duals_ref[channel])
        base[channel] = jnp.zeros(base.shape[1:], F32)
        jones_cur[channel] = jnp.zeros(jones_cur.shape[1:], F32)
        for c in range(8):
            base[channel, c, :, 0:stations] = turned[:, c, :].T
            jones_cur[channel, c, :, 0:stations] = jones_ref[channel, :, c, :].T

    def coherency(channel, group, comp, first):
        if isinstance(group, int) and group == full:
            return coh_tail[channel, comp, first : first + 16, :].astype(F32)
        lanes = pl.ds(pl.multiple_of(group * GROUP, GROUP), GROUP)
        return coh_ref[channel, comp, first : first + 16, lanes].astype(F32)

    def scatter_part(channel, group, side):
        lanes = slice(2 * side * GROUP, 2 * (side + 1) * GROUP)
        update_now[channel][...] += lax.dot_general(
            grad_parts[channel][:, lanes], spread_hot[group, :, lanes], (((1,), (1,)), ((), ())),
            preferred_element_type=F32,
        )

    def scatter(channel, group):
        for side in range(2):
            scatter_part(channel, group, side)

    def stations_of(side, group):
        lanes = pl.ds(group * GROUP if isinstance(group, int) else pl.multiple_of(group * GROUP, GROUP), GROUP)
        return jnp.broadcast_to(jnp.maximum(pairs_pad[side : side + 1, lanes], 0), (8, GROUP))

    def fetch(channel, which, first_row, depth):
        for row in range(first_row, first_row + depth, 8):
            for c in range(8):
                table = jones_cur[channel, c, row : row + 8, :]
                for side in range(2):
                    both_now[channel][c * dirs + row : c * dirs + row + 8, side * GROUP : (side + 1) * GROUP] = (
                        jnp.take_along_axis(table, which[side], axis=1)
                    )

    def visit(channel, group, factor, following=None, between=(None, None, None)):
        both, propagated_ref, parts = both_now[channel], propagated_now[channel], grad_parts[channel]
        lanes = pl.ds(group * GROUP if isinstance(group, int) else pl.multiple_of(group * GROUP, GROUP), GROUP)
        total = None
        for first_row in range(0, dirs, 16):
            wide = [coherency(channel, group, c, first_row) for c in range(8)]
            for upper in range(2):
                at = [slice(c * dirs + first_row + 8 * upper, c * dirs + first_row + 8 * upper + 8) for c in range(8)]
                source = [w[8 * upper : 8 * upper + 8] for w in wide]
                first = [both[at[c], 0:GROUP] for c in range(8)]
                propagated = product(first, source)
                for c in range(8):
                    propagated_ref[at[c], :] = propagated[c]
                second = [both[at[c], GROUP : 2 * GROUP] for c in range(8)]
                model = product_adjoint(propagated, second)
                total = model if total is None else [t + m for t, m in zip(total, model)]
        if between[0]:
            between[0]()
        lanes = pl.ds(pl.multiple_of(group * GROUP, GROUP), GROUP)
        residual = []
        for c in range(8):
            observed = vis_pad[channel, c : c + 1, lanes]
            value = (observed - jnp.sum(total[c], axis=0, keepdims=True)) * factor
            residual.append(jnp.broadcast_to(value, (16, GROUP)))
        place = [slice(n * GROUP, (n + 1) * GROUP) for n in range(4)]
        if following:
            which = [stations_of(side, following[1]) for side in range(2)]
        for first_row in range(0, dirs, 16):
            at = [slice(c * dirs + first_row, c * dirs + first_row + 16) for c in range(8)]
            source = [coherency(channel, group, c, first_row) for c in range(8)]
            second = [both[at[c], GROUP : 2 * GROUP] for c in range(8)]
            conjugated = product_adjoint(second, source)
            for c, value in enumerate(product_terms(residual, conjugated)):
                parts[at[c], place[0]], parts[at[c], place[1]] = split(value)
            propagated = [propagated_ref[at[c], :] for c in range(8)]
            for c, value in enumerate(adjoint_product_terms(residual, propagated)):
                parts[at[c], place[2]], parts[at[c], place[3]] = split(value)
            if following:
                fetch(following[0], which, first_row, 16)
            if between[1] and first_row == dirs // 2 - 16:
                between[1]()
        if between[2]:
            between[2]()

    factors = [counts_ref[channel].astype(F32) * (2.0 * ETA_STEP / SAMPLES) for channel in range(own)]

    def step(_, carry):
        for channel in range(own):
            update_now[channel][...] = jnp.zeros((rows, GROUP), F32)
        grad_parts[1][...] = jnp.zeros(grad_parts[1].shape, BF16)

        fetch(0, [stations_of(side, 0) for side in range(2)], 0, dirs)

        def sweep(group, carry):
            before = jnp.maximum(group - 1, 0)
            visit(0, group, factors[0], (1, group), [
                None, None, lambda: scatter(1, before)
            ])
            visit(1, group, factors[1], (0, group + 1), [
                None, None, lambda: scatter(0, group)
            ])
            return carry

        lax.fori_loop(0, groups - 1, sweep, 0)
        last = groups - 1
        visit(0, last, factors[0], (1, last))
        scatter(1, last - 1)
        visit(1, last, factors[1])
        scatter(0, last)
        scatter(1, last)
        for channel in range(own):
            update = update_now[channel][...].reshape(8, dirs, GROUP)
            jones_cur[channel] = (1.0 - ETA_STEP * RHO_PENALTY) * jones_cur[channel] + base[channel] + update
        return carry

    lax.fori_loop(0, STEPS, step, 0)

    for channel in range(own):
        for c in range(8):
            jones_out[channel, :, c, :] = jones_cur[channel, c].T[0:stations]
    near = stations // 2
    joined = [jones_out[channel] + duals_ref[channel] * (1.0 / RHO_PENALTY) for channel in range(own)]
    for i in range(3):
        value = sum(basis[channel][i] * joined[channel] for channel in range(own))
        sums_out[0:near, i] = jnp.concatenate([value[0:near], value[near : 2 * near]], axis=2)
        sums_out[near, i] = jnp.zeros((8, GROUP), F32)
    agree_kernel(channels, blocks, inverse, sums_out, jones_out, duals_ref, consensus_out, duals_out, *links)


def descend(channels, blocks, pairs, counts, jones, duals, consensus, visibilities, coherencies):
    own, stations, _, dirs = jones.shape
    count = pairs.shape[1]
    groups = -(-count // GROUP)
    lanes = groups * GROUP
    rows = 8 * dirs
    unit = (3, 8, GROUP)
    planes = SIDE * SIDE
    dma = pltpu.SemaphoreType.DMA
    inverse = [[float(v) for v in row] for row in gram_inverse(channels).astype(np.float32)]
    vmem = pl.BlockSpec(memory_space=pltpu.VMEM)
    smem = pl.BlockSpec(memory_space=pltpu.SMEM)
    return pl.pallas_call(
        functools.partial(descend_kernel, channels, blocks, inverse),
        out_shape=tuple(jax.ShapeDtypeStruct(a.shape, F32) for a in (jones, duals, consensus)),
        in_specs=[vmem, smem, vmem, vmem, vmem, vmem, vmem],
        out_specs=(vmem, vmem, vmem),
        scratch_shapes=[
            pltpu.VMEM((stations // 2 + 1,) + unit, F32),
            pltpu.VMEM((8, lanes), jnp.int32),
            pltpu.VMEM((own, 8, lanes), F32),
            pltpu.VMEM((own, 8, dirs, GROUP), BF16),
            pltpu.VMEM((groups, GROUP, 4 * GROUP), BF16),
            pltpu.VMEM((own, 8, dirs, GROUP), F32),
            pltpu.VMEM((own, 8, dirs, GROUP), F32),
            pltpu.VMEM((stations, 8, dirs), F32),
            [pltpu.VMEM((rows, 2 * GROUP), F32)] * own,
            [pltpu.VMEM((rows, GROUP), F32)] * own,
            [pltpu.VMEM((rows, 4 * GROUP), BF16)] * own,
            [pltpu.VMEM((rows, GROUP), F32)] * own,
        ]
        + [pltpu.VMEM((planes,) + unit, F32)] * 3
        + [pltpu.VMEM((SIDE,) + unit, F32), pltpu.VMEM((2 * planes,) + unit, F32)]
        + [dma((planes,))] * 4
        + [dma((SIDE,))] * 2
        + [dma((planes,))] * 4,
        compiler_params=pltpu.CompilerParams(
            collective_id=0, has_side_effects=True, vmem_limit_bytes=28 * 2**20
        ),
        name="descend",
    )(pairs, counts, jones, duals, consensus, visibilities, coherencies)


def agree_kernel(
    channels, blocks, inverse, s_ref, jones_ref, duals_ref, consensus_out, duals_out,
    recv_core, mid, recv_plane, recv_col, full, s1, r1, s2, r2, s3, r3, s4, r4, s5, r5,
):
    z = lax.axis_index("grp"); chan = lax.axis_index("chan")
    core = chan % 2; u = chan // 2; x = u // SIDE; y = u % SIDE
    other = 1 - core
    def peer(dx, dy):
        return ((x + dx) % SIDE) * SIDE + (y + dy) % SIDE
    steps = sorted([(dx, dy) for dx in range(SIDE) for dy in range(SIDE) if dx or dy], key=lambda s: -(min(s[0],4-s[0])+min(s[1],4-s[1])))
    def back(dx, dy):
        return ((x - dx + SIDE) % SIDE) * SIDE + (y - dy + SIDE) % SIDE
    def dev(uu, cc): return {"grp": z, "chan": uu * 2 + cc}
    greet(True)
    order = steps + [(0, 0)]
    def rc(src, dst, ss, rs, d):
        return pltpu.make_async_remote_copy(src_ref=src, dst_ref=dst, send_sem=ss, recv_sem=rs, device_id=d, device_id_type=MESH)
    c1 = []
    for n, (dx, dy) in enumerate(order):
        c = rc(s_ref.at[other * 16 + peer(dx, dy)], recv_core.at[n], s1.at[n], r1.at[n], dev(u, other))
        c.start(); c1.append(c)
    c2 = []
    for n, (dx, dy) in enumerate(order):
        c1[n].wait_recv()
        mid[n] = s_ref[core * 16 + peer(dx, dy)] + recv_core[n]
        if n < 15:
            c = rc(mid.at[n], recv_plane.at[n], s2.at[n], r2.at[n], dev(peer(dx, dy), core))
            c.start(); c2.append(c)
    total = mid[15]
    for n in range(15):
        c2[n].wait_recv()
        total = total + recv_plane[n]
    recv_col[z] = total
    c3 = []
    for dz in range(1, SIDE):
        c = rc(recv_col.at[z], recv_col.at[z], s3.at[dz], r3.at[dz], {"grp": (z + dz) % SIDE, "chan": chan})
        c.start(); c3.append(c)
    for c in c3: c.wait_recv()
    total = recv_col[0] + recv_col[1] + recv_col[2] + recv_col[3]
    mine = core * 16 + u
    for i in range(3):
        full[mine, i] = sum(inverse[i][j] * total[j] for j in range(3))
    c4 = []
    for n, (dx, dy) in enumerate(steps):
        c = rc(full.at[mine], full.at[mine], s4.at[n], r4.at[n], dev(peer(dx, dy), core))
        c.start(); c4.append(c)
    c5 = []
    c = rc(full.at[mine], full.at[mine], s5.at[15], r5.at[15], dev(u, other))
    c.start(); c5.append(c)
    for n, (dx, dy) in reversed(list(enumerate(steps))):
        c4[n].wait_recv()
        unit = core * 16 + back(dx, dy)
        c = rc(full.at[unit], full.at[unit], s5.at[n], r5.at[n], dev(u, other))
        c.start(); c5.append(c)
    for c in c5: c.wait_recv()
    for c in c1 + c2 + c3 + c4 + c5: c.wait_send()
    own, stations, _, dirs = jones_ref.shape
    near = stations // 2
    for i in range(3):
        consensus_out[i, 0:near] = full[0:near, i, :, 0:dirs]
        consensus_out[i, near : 2 * near] = full[0:near, i, :, dirs : 2 * dirs]
    offset = (z * blocks + chan) * own
    for channel in range(own):
        basis = bernstein(((offset + channel).astype(F32) + 0.5) * (1.0 / channels))
        smooth = sum(basis[i] * consensus_out[i] for i in range(3))
        duals_out[channel] = duals_ref[channel] + RHO_PENALTY * (jones_ref[channel] - smooth)


def shards(jones_start, duals_start, consensus_start, visibilities, coherencies, pairs, counts):
    blocks = lax.axis_size("chan")
    channels = jones_start.shape[0] * lax.axis_size("grp") * blocks
    jones, duals, consensus = (jnp.transpose(a, (0, 3, 1, 2)) for a in (jones_start, duals_start, consensus_start))
    outs = descend(channels, blocks, pairs, counts, jones, duals, consensus, visibilities, coherencies)
    return tuple(jnp.transpose(a, (0, 2, 3, 1)) for a in outs)


def solution(mesh):
    in_specs = (
        P(("grp", "chan"), None, None, None),
        P(("grp", "chan"), None, None, None),
        P(),
        P(("grp", "chan"), None, None),
        P(("grp", "chan"), None, None, None),
        P(),
        P(("grp", "chan")),
    )
    out_specs = (P(("grp", "chan"), None, None, None), P(("grp", "chan"), None, None, None), P())
    return jax.shard_map(shards, mesh=mesh, in_specs=in_specs, out_specs=out_specs, check_vma=False)
```

```python
import functools

import jax
import jax.numpy as jnp
import numpy as np
from jax import lax
from jax.experimental import pallas as pl
from jax.experimental.pallas import tpu as pltpu
from jax.sharding import PartitionSpec as P

SAMPLES = 16
STEPS = 2
ETA_STEP = 0.08
RHO_PENALTY = 1.0
GROUP = 128
F32 = jnp.float32
BF16 = jnp.bfloat16
MESH = pl.DeviceIdType.MESH
SIDE = 4


def bernstein(position):
    return [
        (1.0 - position) * (1.0 - position),
        2.0 * position * (1.0 - position),
        position * position,
    ]


def gram_inverse(channels):
    position = (np.arange(channels, dtype=np.float64) + 0.5) / channels
    values = np.stack(bernstein(position))
    matrix = values @ values.T
    rows = [np.cross(matrix[1], matrix[2]), np.cross(matrix[2], matrix[0]), np.cross(matrix[0], matrix[1])]
    return np.stack(rows).T / np.sum(matrix[0] * rows[0])


def triple(entry):
    return entry[0], entry[1] - entry[0], entry[0] + entry[1]


def total_of(values):
    return functools.reduce(lambda former, latter: former + latter, values)


def plain(factors):
    first = total_of([a[2] * b[0] for a, b in factors])
    return first - total_of([a[1] * b[2] for a, b in factors]), first + total_of([a[0] * b[1] for a, b in factors])


def conjugated(factors):
    return (
        total_of([a[2] * b[0] for a, b in factors]),
        total_of([a[1] * b[1] for a, b in factors]),
        total_of([a[0] * b[2] for a, b in factors]),
    )


def entries(values):
    return [(values[2 * n], values[2 * n + 1]) for n in range(4)]


def with_sum(entry):
    return entry[0], entry[1], entry[0] + entry[1]


def split(value):
    high = value.astype(BF16)
    low = (value - high.astype(F32)).astype(BF16)
    return high, low


def greet(wait):
    barrier = pltpu.get_barrier_semaphore()
    z, chan = lax.axis_index("grp"), lax.axis_index("chan")
    core, u = chan % 2, chan // 2
    if wait:
        pl.semaphore_wait(barrier, 1 + SIDE * SIDE - 1 + SIDE - 1)
        return
    pl.semaphore_signal(barrier, inc=1, device_id={"grp": z, "chan": u * 2 + 1 - core}, device_id_type=MESH)
    for dx in range(SIDE):
        for dy in range(SIDE):
            if dx or dy:
                there = ((u // SIDE + dx) % SIDE) * SIDE + (u % SIDE + dy) % SIDE
                pl.semaphore_signal(
                    barrier, inc=1, device_id={"grp": z, "chan": there * 2 + core}, device_id_type=MESH
                )
    for dz in range(1, SIDE):
        pl.semaphore_signal(barrier, inc=1, device_id={"grp": (z + dz) % SIDE, "chan": chan}, device_id_type=MESH)


def descend_kernel(
    channels, blocks, inverse, pairs_in, counts_ref, jones_in, duals_in, consensus_in, vis_in, coh_in,
    jones_out, duals_out, consensus_out, sums_out,
    pairs_pad, vis_pad, coh_tail, spread_hot, jones_cur, base, turned, both_now,
    propagated_now, turned_now, grad_parts, update_now, pairs_ref, jones_ref, duals_ref, consensus_ref, vis_ref, coh_ref,
    arrived, *links,
):
    own, stations, _, dirs = jones_ref.shape
    count = pairs_ref.shape[1]
    groups = spread_hot.shape[0]
    full = count // GROUP
    rows = 8 * dirs
    offset = (lax.axis_index("grp") * blocks + lax.axis_index("chan")) * own

    greet(False)
    inputs = [
        (pairs_in, pairs_ref), (vis_in, vis_ref), (consensus_in, consensus_ref), (duals_in, duals_ref),
        (jones_in, jones_ref), (coh_in, coh_ref),
    ]
    inputs = [pltpu.make_async_copy(a, b, arrived.at[n]) for n, (a, b) in enumerate(inputs)]
    for copy in inputs:
        copy.start()

    pairs_pad[...] = jnp.full(pairs_pad.shape, -1, jnp.int32)
    inputs[0].wait()
    pairs_pad[0:2, 0:count] = pairs_ref[...]

    ids = lax.broadcasted_iota(jnp.int32, (GROUP, GROUP), 0)
    for group in range(groups):
        for side in range(2):
            row = pairs_pad[side : side + 1, group * GROUP : (group + 1) * GROUP]
            hot = jnp.where(ids == row, 1.0, 0.0).astype(BF16)
            for part in range(2):
                where = (2 * side + part) * GROUP
                spread_hot[group, :, where : where + GROUP] = hot

    inputs[1].wait()
    vis_pad[...] = jnp.zeros(vis_pad.shape, F32)
    vis_pad[:, :, 0:count] = vis_ref[...]
    for copy in inputs[2:5]:
        copy.wait()

    basis = []
    for channel in range(own):
        position = ((offset + channel).astype(F32) + 0.5) * (1.0 / channels)
        basis.append(bernstein(position))
        target = sum(basis[channel][i] * consensus_ref[i] for i in range(3))
        turned[channel] = ETA_STEP * (RHO_PENALTY * target - duals_ref[channel])
        base[channel] = jnp.zeros(base.shape[1:], F32)
        jones_cur[channel] = jnp.zeros(jones_cur.shape[1:], F32)
        for c in range(8):
            jones_cur[channel, c, :, 0:stations] = jones_ref[channel, :, c, :].T

    def turn(channel):
        for c in range(8):
            base[channel, c, :, 0:stations] = turned[channel, :, c, :].T

    def coherency(channel, group, comp, first):
        if isinstance(group, int) and group == full:
            return coh_tail[channel, comp, first : first + 16, :].astype(F32)
        lanes = pl.ds(pl.multiple_of(group * GROUP, GROUP), GROUP)
        return coh_ref[channel, comp, first : first + 16, lanes].astype(F32)

    def scatter_part(channel, group, side):
        lanes = slice(2 * side * GROUP, 2 * (side + 1) * GROUP)
        update_now[channel][...] += lax.dot_general(
            grad_parts[channel][:, lanes], spread_hot[group, :, lanes], (((1,), (1,)), ((), ())),
            preferred_element_type=F32,
        )

    def scatter(channel, group):
        for side in range(2):
            scatter_part(channel, group, side)

    def stations_of(side, group):
        lanes = pl.ds(group * GROUP if isinstance(group, int) else pl.multiple_of(group * GROUP, GROUP), GROUP)
        return jnp.broadcast_to(jnp.maximum(pairs_pad[side : side + 1, lanes], 0), (8, GROUP))

    def fetch(channel, which, first_row, depth):
        for row in range(first_row, first_row + depth, 8):
            for c in range(8):
                table = jones_cur[channel, c, row : row + 8, :]
                for side in range(2):
                    both_now[channel][c * dirs + row : c * dirs + row + 8, side * GROUP : (side + 1) * GROUP] = (
                        jnp.take_along_axis(table, which[side], axis=1)
                    )

    def visit(channel, group, factor, following=None, between=(None, None, None)):
        both, propagated_ref, turned_ref = both_now[channel], propagated_now[channel], turned_now[channel]
        parts = grad_parts[channel]
        lanes = pl.ds(group * GROUP if isinstance(group, int) else pl.multiple_of(group * GROUP, GROUP), GROUP)
        total = None
        for first_row in range(0, dirs, 16):
            wide = [coherency(channel, group, c, first_row) for c in range(8)]
            for upper in range(2):
                at = [slice(c * dirs + first_row + 8 * upper, c * dirs + first_row + 8 * upper + 8) for c in range(8)]
                source = [with_sum(e) for e in entries([w[8 * upper : 8 * upper + 8] for w in wide])]
                first = [triple(e) for e in entries([both[at[c], 0:GROUP] for c in range(8)])]
                propagated = []
                for row in range(2):
                    for col in range(2):
                        value = plain([(source[2 * m + col], first[2 * row + m]) for m in range(2)])
                        for part in range(2):
                            propagated_ref[at[2 * (2 * row + col) + part], :] = value[part]
                        propagated.append(with_sum(value))
                second = [triple(e) for e in entries([both[at[c], GROUP : 2 * GROUP] for c in range(8)])]
                model = []
                for row in range(2):
                    for col in range(2):
                        model.extend(conjugated([(propagated[2 * row + n], second[2 * col + n]) for n in range(2)]))
                total = model if total is None else [t + m for t, m in zip(total, model)]
                for row in range(2):
                    for col in range(2):
                        one, two, three = conjugated([(source[2 * col + n], second[2 * row + n]) for n in range(2)])
                        turned_ref[at[2 * (2 * row + col)], :] = one + two
                        turned_ref[at[2 * (2 * row + col) + 1], :] = three - one
        if between[0]:
            between[0]()
        lanes = pl.ds(pl.multiple_of(group * GROUP, GROUP), GROUP)
        residual = []
        for n in range(4):
            sums = [jnp.sum(total[3 * n + part], axis=0, keepdims=True) for part in range(3)]
            pair = (sums[0] + sums[1], sums[0] - sums[2])
            observed = [vis_pad[channel, 2 * n + part : 2 * n + part + 1, lanes] for part in range(2)]
            pair = triple([(observed[part] - pair[part]) * factor for part in range(2)])
            residual.append([jnp.broadcast_to(value, (16, GROUP)) for value in pair])
        place = [slice(n * GROUP, (n + 1) * GROUP) for n in range(4)]
        if following:
            which = [stations_of(side, following[1]) for side in range(2)]
        for first_row in range(0, dirs, 16):
            at = [slice(c * dirs + first_row, c * dirs + first_row + 16) for c in range(8)]
            turned_jones = [with_sum(e) for e in entries([turned_ref[at[c], :] for c in range(8)])]
            for row in range(2):
                for col in range(2):
                    value = plain([(turned_jones[2 * b + col], residual[2 * row + b]) for b in range(2)])
                    for part in range(2):
                        where = at[2 * (2 * row + col) + part]
                        parts[where, place[0]], parts[where, place[1]] = split(value[part])
            propagated = [with_sum(e) for e in entries([propagated_ref[at[c], :] for c in range(8)])]
            for row in range(2):
                for col in range(2):
                    one, two, three = conjugated([(propagated[2 * a + col], residual[2 * a + row]) for a in range(2)])
                    for part, value in enumerate((one + two, one - three)):
                        where = at[2 * (2 * row + col) + part]
                        parts[where, place[2]], parts[where, place[3]] = split(value)
            if following:
                fetch(following[0], which, first_row, 16)
            if between[1] and first_row == dirs // 2 - 16:
                between[1]()
        if between[2]:
            between[2]()

    inputs[5].wait()
    coh_tail[...] = jnp.zeros(coh_tail.shape, BF16)
    coh_tail[:, :, :, 0 : count - full * GROUP] = coh_ref[:, :, :, full * GROUP : count]
    factors = [counts_ref[channel].astype(F32) * (2.0 * ETA_STEP / SAMPLES) for channel in range(own)]

    def step(_, carry):
        for channel in range(own):
            update_now[channel][...] = jnp.zeros((rows, GROUP), F32)
        grad_parts[1][...] = jnp.zeros(grad_parts[1].shape, BF16)

        fetch(0, [stations_of(side, 0) for side in range(2)], 0, dirs)

        def sweep(group, carry):
            before = jnp.maximum(group - 1, 0)
            visit(0, group, factors[0], (1, group), [
                None, None, lambda: scatter(1, before)
            ])
            visit(1, group, factors[1], (0, group + 1), [
                None, None, lambda: scatter(0, group)
            ])
            return carry

        lax.fori_loop(0, groups - 1, sweep, 0)
        last = groups - 1
        visit(0, last, factors[0], (1, last))
        scatter(1, last - 1)
        turn(0)
        visit(1, last, factors[1], None, [None, lambda: turn(1), None])
        scatter(0, last)
        scatter(1, last)
        for channel in range(own):
            update = update_now[channel][...].reshape(8, dirs, GROUP)
            jones_cur[channel] = (1.0 - ETA_STEP * RHO_PENALTY) * jones_cur[channel] + base[channel] + update
        return carry

    lax.fori_loop(0, STEPS, step, 0)

    for channel in range(own):
        for c in range(8):
            jones_out[channel, :, c, :] = jones_cur[channel, c].T[0:stations]
    near = stations // 2
    joined = [jones_out[channel] + duals_ref[channel] * (1.0 / RHO_PENALTY) for channel in range(own)]
    for i in range(3):
        value = sum(basis[channel][i] * joined[channel] for channel in range(own))
        sums_out[0:near, i] = jnp.concatenate([value[0:near], value[near : 2 * near]], axis=2)
        sums_out[near, i] = jnp.zeros((8, GROUP), F32)
    agree_kernel(channels, blocks, inverse, sums_out, jones_out, duals_ref, consensus_out, duals_out, *links)


def descend(channels, blocks, pairs, counts, jones, duals, consensus, visibilities, coherencies):
    own, stations, _, dirs = jones.shape
    count = pairs.shape[1]
    groups = -(-count // GROUP)
    lanes = groups * GROUP
    rows = 8 * dirs
    unit = (3, 8, GROUP)
    planes = SIDE * SIDE
    dma = pltpu.SemaphoreType.DMA
    inverse = [[float(v) for v in row] for row in gram_inverse(channels).astype(np.float32)]
    vmem = pl.BlockSpec(memory_space=pltpu.VMEM)
    smem = pl.BlockSpec(memory_space=pltpu.SMEM)
    anywhere = pl.BlockSpec(memory_space=pl.ANY)
    return pl.pallas_call(
        functools.partial(descend_kernel, channels, blocks, inverse),
        out_shape=tuple(jax.ShapeDtypeStruct(a.shape, F32) for a in (jones, duals, consensus)),
        in_specs=[anywhere, smem] + [anywhere] * 5,
        out_specs=(vmem, vmem, vmem),
        scratch_shapes=[
            pltpu.VMEM((stations // 2 + 1,) + unit, F32),
            pltpu.VMEM((8, lanes), jnp.int32),
            pltpu.VMEM((own, 8, lanes), F32),
            pltpu.VMEM((own, 8, dirs, GROUP), BF16),
            pltpu.VMEM((groups, GROUP, 4 * GROUP), BF16),
            pltpu.VMEM((own, 8, dirs, GROUP), F32),
            pltpu.VMEM((own, 8, dirs, GROUP), F32),
            pltpu.VMEM((own, stations, 8, dirs), F32),
            [pltpu.VMEM((rows, 2 * GROUP), F32)] * own,
            [pltpu.VMEM((rows, GROUP), F32)] * own,
            [pltpu.VMEM((rows, GROUP), F32)] * own,
            [pltpu.VMEM((rows, 4 * GROUP), BF16)] * own,
            [pltpu.VMEM((rows, GROUP), F32)] * own,
        ]
        + [pltpu.VMEM(a.shape, a.dtype) for a in (pairs, jones, duals, consensus, visibilities, coherencies)]
        + [dma((6,))]
        + [pltpu.VMEM((planes,) + unit, F32)] * 3
        + [pltpu.VMEM((SIDE,) + unit, F32), pltpu.VMEM((2 * planes,) + unit, F32)]
        + [dma((planes,))] * 4
        + [dma((SIDE,))] * 2
        + [dma((planes,))] * 4,
        compiler_params=pltpu.CompilerParams(
            collective_id=0, has_side_effects=True, vmem_limit_bytes=56 * 2**20
        ),
        name="descend",
    )(pairs, counts, jones, duals, consensus, visibilities, coherencies)


def agree_kernel(
    channels, blocks, inverse, s_ref, jones_ref, duals_ref, consensus_out, duals_out,
    recv_core, mid, recv_plane, recv_col, full, s1, r1, s2, r2, s3, r3, s4, r4, s5, r5,
):
    z = lax.axis_index("grp"); chan = lax.axis_index("chan")
    core = chan % 2; u = chan // 2; x = u // SIDE; y = u % SIDE
    other = 1 - core
    def peer(dx, dy):
        return ((x + dx) % SIDE) * SIDE + (y + dy) % SIDE
    steps = sorted([(dx, dy) for dx in range(SIDE) for dy in range(SIDE) if dx or dy], key=lambda s: -(min(s[0],4-s[0])+min(s[1],4-s[1])))
    def back(dx, dy):
        return ((x - dx + SIDE) % SIDE) * SIDE + (y - dy + SIDE) % SIDE
    def dev(uu, cc): return {"grp": z, "chan": uu * 2 + cc}
    greet(True)
    order = steps + [(0, 0)]
    def rc(src, dst, ss, rs, d):
        return pltpu.make_async_remote_copy(src_ref=src, dst_ref=dst, send_sem=ss, recv_sem=rs, device_id=d, device_id_type=MESH)
    c1 = []
    for n, (dx, dy) in enumerate(order):
        c = rc(s_ref.at[other * 16 + peer(dx, dy)], recv_core.at[n], s1.at[n], r1.at[n], dev(u, other))
        c.start(); c1.append(c)
    c2 = []
    for n, (dx, dy) in enumerate(order):
        c1[n].wait_recv()
        mid[n] = s_ref[core * 16 + peer(dx, dy)] + recv_core[n]
        if n < 15:
            c = rc(mid.at[n], recv_plane.at[n], s2.at[n], r2.at[n], dev(peer(dx, dy), core))
            c.start(); c2.append(c)
    total = mid[15]
    for n in range(15):
        c2[n].wait_recv()
        total = total + recv_plane[n]
    recv_col[z] = total
    c3 = []
    for dz in range(1, SIDE):
        c = rc(recv_col.at[z], recv_col.at[z], s3.at[dz], r3.at[dz], {"grp": (z + dz) % SIDE, "chan": chan})
        c.start(); c3.append(c)
    for c in c3: c.wait_recv()
    total = recv_col[0] + recv_col[1] + recv_col[2] + recv_col[3]
    mine = core * 16 + u
    for i in range(3):
        full[mine, i] = sum(inverse[i][j] * total[j] for j in range(3))
    c4 = []
    for n, (dx, dy) in enumerate(steps):
        c = rc(full.at[mine], full.at[mine], s4.at[n], r4.at[n], dev(peer(dx, dy), core))
        c.start(); c4.append(c)
    c5 = []
    c = rc(full.at[mine], full.at[mine], s5.at[15], r5.at[15], dev(u, other))
    c.start(); c5.append(c)
    for n, (dx, dy) in reversed(list(enumerate(steps))):
        c4[n].wait_recv()
        unit = core * 16 + back(dx, dy)
        c = rc(full.at[unit], full.at[unit], s5.at[n], r5.at[n], dev(u, other))
        c.start(); c5.append(c)
    own, stations, _, dirs = jones_ref.shape
    near = stations // 2
    offset = (z * blocks + chan) * own
    basis = [bernstein(((offset + channel).astype(F32) + 0.5) * (1.0 / channels)) for channel in range(own)]

    def finish(unit):
        @pl.when(unit < near)
        def _():
            for side in range(2):
                station = unit + side * near
                agreed = [full[unit, i, :, side * dirs : (side + 1) * dirs] for i in range(3)]
                for i in range(3):
                    consensus_out[i, station] = agreed[i]
                for channel in range(own):
                    smooth = sum(basis[channel][i] * agreed[i] for i in range(3))
                    duals_out[channel, station] = duals_ref[channel, station] + RHO_PENALTY * (
                        jones_ref[channel, station] - smooth
                    )

    finish(mine)
    for dx, dy in reversed(steps):
        finish(core * 16 + back(dx, dy))
    for n, c in enumerate(c5):
        c.wait_recv()
        dx, dy = ([(0, 0)] + list(reversed(steps)))[n]
        finish(other * 16 + back(dx, dy))
    for c in c1 + c2 + c3 + c4 + c5: c.wait_send()


def shards(jones_start, duals_start, consensus_start, visibilities, coherencies, pairs, counts):
    blocks = lax.axis_size("chan")
    channels = jones_start.shape[0] * lax.axis_size("grp") * blocks
    jones, duals, consensus = (jnp.transpose(a, (0, 3, 1, 2)) for a in (jones_start, duals_start, consensus_start))
    outs = descend(channels, blocks, pairs, counts, jones, duals, consensus, visibilities, coherencies)
    return tuple(jnp.transpose(a, (0, 2, 3, 1)) for a in outs)


def solution(mesh):
    in_specs = (
        P(("grp", "chan"), None, None, None),
        P(("grp", "chan"), None, None, None),
        P(),
        P(("grp", "chan"), None, None),
        P(("grp", "chan"), None, None, None),
        P(),
        P(("grp", "chan")),
    )
    out_specs = (P(("grp", "chan"), None, None, None), P(("grp", "chan"), None, None, None), P())
    return jax.shard_map(shards, mesh=mesh, in_specs=in_specs, out_specs=out_specs, check_vma=False)
```

```python
import functools

import jax
import jax.numpy as jnp
import numpy as np
from jax import lax
from jax.experimental import pallas as pl
from jax.experimental.pallas import tpu as pltpu
from jax.sharding import PartitionSpec as P

SAMPLES = 16
STEPS = 2
ETA_STEP = 0.08
RHO_PENALTY = 1.0
GROUP = 128
F32 = jnp.float32
BF16 = jnp.bfloat16
MESH = pl.DeviceIdType.MESH
SIDE = 4


def bernstein(position):
    return [
        (1.0 - position) * (1.0 - position),
        2.0 * position * (1.0 - position),
        position * position,
    ]


def gram_inverse(channels):
    position = (np.arange(channels, dtype=np.float64) + 0.5) / channels
    values = np.stack(bernstein(position))
    matrix = values @ values.T
    rows = [np.cross(matrix[1], matrix[2]), np.cross(matrix[2], matrix[0]), np.cross(matrix[0], matrix[1])]
    return np.stack(rows).T / np.sum(matrix[0] * rows[0])


def triple(entry):
    return entry[0], entry[1] - entry[0], entry[0] + entry[1]


def total_of(values):
    return functools.reduce(lambda former, latter: former + latter, values)


def plain(factors):
    first = total_of([a[2] * b[0] for a, b in factors])
    return first - total_of([a[1] * b[2] for a, b in factors]), first + total_of([a[0] * b[1] for a, b in factors])


def conjugated(factors):
    return (
        total_of([a[2] * b[0] for a, b in factors]),
        total_of([a[1] * b[1] for a, b in factors]),
        total_of([a[0] * b[2] for a, b in factors]),
    )


def entries(values):
    return [(values[2 * n], values[2 * n + 1]) for n in range(4)]


def with_sum(entry):
    return entry[0], entry[1], entry[0] + entry[1]


def split(value):
    high = value.astype(BF16)
    low = (value - high.astype(F32)).astype(BF16)
    return high, low


def greet(wait):
    barrier = pltpu.get_barrier_semaphore()
    z, chan = lax.axis_index("grp"), lax.axis_index("chan")
    core, u = chan % 2, chan // 2
    if wait:
        pl.semaphore_wait(barrier, 1 + SIDE * SIDE - 1 + SIDE - 1)
        return
    pl.semaphore_signal(barrier, inc=1, device_id={"grp": z, "chan": u * 2 + 1 - core}, device_id_type=MESH)
    for dx in range(SIDE):
        for dy in range(SIDE):
            if dx or dy:
                there = ((u // SIDE + dx) % SIDE) * SIDE + (u % SIDE + dy) % SIDE
                pl.semaphore_signal(
                    barrier, inc=1, device_id={"grp": z, "chan": there * 2 + core}, device_id_type=MESH
                )
    for dz in range(1, SIDE):
        pl.semaphore_signal(barrier, inc=1, device_id={"grp": (z + dz) % SIDE, "chan": chan}, device_id_type=MESH)


def descend_kernel(
    channels, blocks, inverse, pairs_in, counts_ref, jones_in, duals_in, consensus_in, vis_in, coh_in,
    jones_out, duals_out, consensus_out, sums_out,
    pairs_pad, vis_pad, coh_tail, spread_hot, jones_cur, base, turned, both_now,
    propagated_now, turned_now, grad_parts, update_now, pairs_ref, jones_ref, duals_ref, consensus_ref, vis_ref, coh_ref,
    arrived, *links,
):
    own, stations, _, dirs = jones_ref.shape
    count = pairs_ref.shape[1]
    groups = spread_hot.shape[0]
    full = count // GROUP
    rows = 8 * dirs
    offset = (lax.axis_index("grp") * blocks + lax.axis_index("chan")) * own

    greet(False)
    inputs = [
        (pairs_in, pairs_ref), (jones_in, jones_ref), (vis_in, vis_ref), (consensus_in, consensus_ref),
        (duals_in, duals_ref),
    ]
    for channel in range(own):
        inputs.extend((coh_in.at[channel, c], coh_ref.at[channel, c]) for c in range(8))
    inputs = [pltpu.make_async_copy(a, b, arrived.at[n]) for n, (a, b) in enumerate(inputs)]
    for copy in inputs:
        copy.start()

    pairs_pad[...] = jnp.full(pairs_pad.shape, -1, jnp.int32)
    inputs[0].wait()
    pairs_pad[0:2, 0:count] = pairs_ref[...]

    ids = lax.broadcasted_iota(jnp.int32, (GROUP, GROUP), 0)
    for group in range(groups):
        for side in range(2):
            row = pairs_pad[side : side + 1, group * GROUP : (group + 1) * GROUP]
            hot = jnp.where(ids == row, 1.0, 0.0).astype(BF16)
            for part in range(2):
                where = (2 * side + part) * GROUP
                spread_hot[group, :, where : where + GROUP] = hot

    inputs[2].wait()
    vis_pad[...] = jnp.zeros(vis_pad.shape, F32)
    vis_pad[:, :, 0:count] = vis_ref[...]
    for copy in (inputs[1], inputs[3], inputs[4]):
        copy.wait()

    basis = []
    for channel in range(own):
        position = ((offset + channel).astype(F32) + 0.5) * (1.0 / channels)
        basis.append(bernstein(position))
        target = sum(basis[channel][i] * consensus_ref[i] for i in range(3))
        turned[channel] = ETA_STEP * (RHO_PENALTY * target - duals_ref[channel])
        base[channel] = jnp.zeros(base.shape[1:], F32)
        jones_cur[channel] = jnp.zeros(jones_cur.shape[1:], F32)
        for c in range(8):
            jones_cur[channel, c, :, 0:stations] = jones_ref[channel, :, c, :].T

    def turn(channel):
        for c in range(8):
            base[channel, c, :, 0:stations] = turned[channel, :, c, :].T

    def coherency(channel, group, comp, first):
        if isinstance(group, int) and group == full:
            return coh_tail[channel, comp, first : first + 16, :].astype(F32)
        lanes = pl.ds(pl.multiple_of(group * GROUP, GROUP), GROUP)
        return coh_ref[channel, comp, first : first + 16, lanes].astype(F32)

    def scatter_part(channel, group, side):
        lanes = slice(2 * side * GROUP, 2 * (side + 1) * GROUP)
        update_now[channel][...] += lax.dot_general(
            grad_parts[channel][:, lanes], spread_hot[group, :, lanes], (((1,), (1,)), ((), ())),
            preferred_element_type=F32,
        )

    def scatter(channel, group):
        for side in range(2):
            scatter_part(channel, group, side)

    def stations_of(side, group):
        lanes = pl.ds(group * GROUP if isinstance(group, int) else pl.multiple_of(group * GROUP, GROUP), GROUP)
        return jnp.broadcast_to(jnp.maximum(pairs_pad[side : side + 1, lanes], 0), (8, GROUP))

    def fetch(channel, which, first_row, depth):
        for row in range(first_row, first_row + depth, 8):
            for c in range(8):
                table = jones_cur[channel, c, row : row + 8, :]
                for side in range(2):
                    both_now[channel][c * dirs + row : c * dirs + row + 8, side * GROUP : (side + 1) * GROUP] = (
                        jnp.take_along_axis(table, which[side], axis=1)
                    )

    def visit(channel, group, factor, following=None, between=(None, None, None)):
        both, propagated_ref, turned_ref = both_now[channel], propagated_now[channel], turned_now[channel]
        parts = grad_parts[channel]
        lanes = pl.ds(group * GROUP if isinstance(group, int) else pl.multiple_of(group * GROUP, GROUP), GROUP)
        total = None
        for first_row in range(0, dirs, 16):
            wide = [coherency(channel, group, c, first_row) for c in range(8)]
            for upper in range(2):
                at = [slice(c * dirs + first_row + 8 * upper, c * dirs + first_row + 8 * upper + 8) for c in range(8)]
                source = [with_sum(e) for e in entries([w[8 * upper : 8 * upper + 8] for w in wide])]
                first = [triple(e) for e in entries([both[at[c], 0:GROUP] for c in range(8)])]
                propagated = []
                for row in range(2):
                    for col in range(2):
                        value = plain([(source[2 * m + col], first[2 * row + m]) for m in range(2)])
                        for part in range(2):
                            propagated_ref[at[2 * (2 * row + col) + part], :] = value[part]
                        propagated.append(with_sum(value))
                second = [triple(e) for e in entries([both[at[c], GROUP : 2 * GROUP] for c in range(8)])]
                model = []
                for row in range(2):
                    for col in range(2):
                        model.extend(conjugated([(propagated[2 * row + n], second[2 * col + n]) for n in range(2)]))
                total = model if total is None else [t + m for t, m in zip(total, model)]
                for row in range(2):
                    for col in range(2):
                        one, two, three = conjugated([(source[2 * col + n], second[2 * row + n]) for n in range(2)])
                        turned_ref[at[2 * (2 * row + col)], :] = one + two
                        turned_ref[at[2 * (2 * row + col) + 1], :] = three - one
        if between[0]:
            between[0]()
        lanes = pl.ds(pl.multiple_of(group * GROUP, GROUP), GROUP)
        residual = []
        for n in range(4):
            sums = [jnp.sum(total[3 * n + part], axis=0, keepdims=True) for part in range(3)]
            pair = (sums[0] + sums[1], sums[0] - sums[2])
            observed = [vis_pad[channel, 2 * n + part : 2 * n + part + 1, lanes] for part in range(2)]
            pair = triple([(observed[part] - pair[part]) * factor for part in range(2)])
            residual.append([jnp.broadcast_to(value, (16, GROUP)) for value in pair])
        place = [slice(n * GROUP, (n + 1) * GROUP) for n in range(4)]
        if following:
            which = [stations_of(side, following[1]) for side in range(2)]
        for first_row in range(0, dirs, 16):
            at = [slice(c * dirs + first_row, c * dirs + first_row + 16) for c in range(8)]
            turned_jones = [with_sum(e) for e in entries([turned_ref[at[c], :] for c in range(8)])]
            for row in range(2):
                for col in range(2):
                    value = plain([(turned_jones[2 * b + col], residual[2 * row + b]) for b in range(2)])
                    for part in range(2):
                        where = at[2 * (2 * row + col) + part]
                        parts[where, place[0]], parts[where, place[1]] = split(value[part])
            propagated = [with_sum(e) for e in entries([propagated_ref[at[c], :] for c in range(8)])]
            for row in range(2):
                for col in range(2):
                    one, two, three = conjugated([(propagated[2 * a + col], residual[2 * a + row]) for a in range(2)])
                    for part, value in enumerate((one + two, one - three)):
                        where = at[2 * (2 * row + col) + part]
                        parts[where, place[2]], parts[where, place[3]] = split(value)
            if following:
                fetch(following[0], which, first_row, 16)
            if between[1] and first_row == dirs // 2 - 16:
                between[1]()
        if between[2]:
            between[2]()

    for copy in inputs[5:]:
        copy.wait()
    coh_tail[...] = jnp.zeros(coh_tail.shape, BF16)
    coh_tail[:, :, :, 0 : count - full * GROUP] = coh_ref[:, :, :, full * GROUP : count]
    factors = [counts_ref[channel].astype(F32) * (2.0 * ETA_STEP / SAMPLES) for channel in range(own)]

    def step(_, carry):
        for channel in range(own):
            update_now[channel][...] = jnp.zeros((rows, GROUP), F32)
        grad_parts[1][...] = jnp.zeros(grad_parts[1].shape, BF16)

        fetch(0, [stations_of(side, 0) for side in range(2)], 0, dirs)

        def sweep(group, carry):
            before = jnp.maximum(group - 1, 0)
            visit(0, group, factors[0], (1, group), [
                None, None, lambda: scatter(1, before)
            ])
            visit(1, group, factors[1], (0, group + 1), [
                None, None, lambda: scatter(0, group)
            ])
            return carry

        lax.fori_loop(0, groups - 1, sweep, 0)
        last = groups - 1
        visit(0, last, factors[0], (1, last))
        scatter(1, last - 1)
        turn(0)
        visit(1, last, factors[1], None, [None, lambda: turn(1), None])
        scatter(0, last)
        scatter(1, last)
        for channel in range(own):
            update = update_now[channel][...].reshape(8, dirs, GROUP)
            jones_cur[channel] = (1.0 - ETA_STEP * RHO_PENALTY) * jones_cur[channel] + base[channel] + update
        return carry

    lax.fori_loop(0, STEPS, step, 0)

    for channel in range(own):
        for c in range(8):
            jones_out[channel, :, c, :] = jones_cur[channel, c].T[0:stations]
    near = stations // 2
    joined = [jones_out[channel] + duals_ref[channel] * (1.0 / RHO_PENALTY) for channel in range(own)]
    for i in range(3):
        value = sum(basis[channel][i] * joined[channel] for channel in range(own))
        sums_out[0:near, i] = jnp.concatenate([value[0:near], value[near : 2 * near]], axis=2)
        sums_out[near, i] = jnp.zeros((8, GROUP), F32)
    agree_kernel(channels, blocks, inverse, sums_out, jones_out, duals_ref, consensus_out, duals_out, *links)


def descend(channels, blocks, pairs, counts, jones, duals, consensus, visibilities, coherencies):
    own, stations, _, dirs = jones.shape
    count = pairs.shape[1]
    groups = -(-count // GROUP)
    lanes = groups * GROUP
    rows = 8 * dirs
    unit = (3, 8, GROUP)
    planes = SIDE * SIDE
    dma = pltpu.SemaphoreType.DMA
    inverse = [[float(v) for v in row] for row in gram_inverse(channels).astype(np.float32)]
    vmem = pl.BlockSpec(memory_space=pltpu.VMEM)
    smem = pl.BlockSpec(memory_space=pltpu.SMEM)
    anywhere = pl.BlockSpec(memory_space=pl.ANY)
    return pl.pallas_call(
        functools.partial(descend_kernel, channels, blocks, inverse),
        out_shape=tuple(pltpu.VMEM(a.shape, F32) for a in (jones, duals, consensus)),
        in_specs=[anywhere, smem] + [anywhere] * 5,
        out_specs=(vmem, vmem, vmem),
        scratch_shapes=[
            pltpu.VMEM((stations // 2 + 1,) + unit, F32),
            pltpu.VMEM((8, lanes), jnp.int32),
            pltpu.VMEM((own, 8, lanes), F32),
            pltpu.VMEM((own, 8, dirs, GROUP), BF16),
            pltpu.VMEM((groups, GROUP, 4 * GROUP), BF16),
            pltpu.VMEM((own, 8, dirs, GROUP), F32),
            pltpu.VMEM((own, 8, dirs, GROUP), F32),
            pltpu.VMEM((own, stations, 8, dirs), F32),
            [pltpu.VMEM((rows, 2 * GROUP), F32)] * own,
            [pltpu.VMEM((rows, GROUP), F32)] * own,
            [pltpu.VMEM((rows, GROUP), F32)] * own,
            [pltpu.VMEM((rows, 4 * GROUP), BF16)] * own,
            [pltpu.VMEM((rows, GROUP), F32)] * own,
        ]
        + [pltpu.VMEM(a.shape, a.dtype) for a in (pairs, jones, duals, consensus, visibilities, coherencies)]
        + [dma((5 + 8 * own,))]
        + [pltpu.VMEM((planes,) + unit, F32)] * 3
        + [pltpu.VMEM((SIDE,) + unit, F32), pltpu.VMEM((2 * planes,) + unit, F32)]
        + [dma((planes,))] * 4
        + [dma((SIDE,))] * 2
        + [dma((planes,))] * 4,
        compiler_params=pltpu.CompilerParams(
            collective_id=0, has_side_effects=True, vmem_limit_bytes=56 * 2**20
        ),
        name="descend",
    )(pairs, counts, jones, duals, consensus, visibilities, coherencies)


def agree_kernel(
    channels, blocks, inverse, s_ref, jones_ref, duals_ref, consensus_out, duals_out,
    recv_core, mid, recv_plane, recv_col, full, s1, r1, s2, r2, s3, r3, s4, r4, s5, r5,
):
    z = lax.axis_index("grp"); chan = lax.axis_index("chan")
    core = chan % 2; u = chan // 2; x = u // SIDE; y = u % SIDE
    other = 1 - core
    def peer(dx, dy):
        return ((x + dx) % SIDE) * SIDE + (y + dy) % SIDE
    steps = sorted([(dx, dy) for dx in range(SIDE) for dy in range(SIDE) if dx or dy], key=lambda s: -(min(s[0],4-s[0])+min(s[1],4-s[1])))
    def back(dx, dy):
        return ((x - dx + SIDE) % SIDE) * SIDE + (y - dy + SIDE) % SIDE
    def dev(uu, cc): return {"grp": z, "chan": uu * 2 + cc}
    greet(True)
    order = steps + [(0, 0)]
    def rc(src, dst, ss, rs, d):
        return pltpu.make_async_remote_copy(src_ref=src, dst_ref=dst, send_sem=ss, recv_sem=rs, device_id=d, device_id_type=MESH)
    c1 = []
    for n, (dx, dy) in enumerate(order):
        c = rc(s_ref.at[other * 16 + peer(dx, dy)], recv_core.at[n], s1.at[n], r1.at[n], dev(u, other))
        c.start(); c1.append(c)
    c2 = []
    for n, (dx, dy) in enumerate(order):
        c1[n].wait_recv()
        mid[n] = s_ref[core * 16 + peer(dx, dy)] + recv_core[n]
        if n < 15:
            c = rc(mid.at[n], recv_plane.at[n], s2.at[n], r2.at[n], dev(peer(dx, dy), core))
            c.start(); c2.append(c)
    total = mid[15]
    for n in range(15):
        c2[n].wait_recv()
        total = total + recv_plane[n]
    recv_col[z] = total
    c3 = []
    for dz in range(1, SIDE):
        c = rc(recv_col.at[z], recv_col.at[z], s3.at[dz], r3.at[dz], {"grp": (z + dz) % SIDE, "chan": chan})
        c.start(); c3.append(c)
    for c in c3: c.wait_recv()
    total = recv_col[0] + recv_col[1] + recv_col[2] + recv_col[3]
    mine = core * 16 + u
    for i in range(3):
        full[mine, i] = sum(inverse[i][j] * total[j] for j in range(3))
    c4 = []
    for n, (dx, dy) in enumerate(steps):
        c = rc(full.at[mine], full.at[mine], s4.at[n], r4.at[n], dev(peer(dx, dy), core))
        c.start(); c4.append(c)
    c5 = []
    c = rc(full.at[mine], full.at[mine], s5.at[15], r5.at[15], dev(u, other))
    c.start(); c5.append(c)
    for n, (dx, dy) in reversed(list(enumerate(steps))):
        c4[n].wait_recv()
        unit = core * 16 + back(dx, dy)
        c = rc(full.at[unit], full.at[unit], s5.at[n], r5.at[n], dev(u, other))
        c.start(); c5.append(c)
    own, stations, _, dirs = jones_ref.shape
    near = stations // 2
    offset = (z * blocks + chan) * own
    basis = [bernstein(((offset + channel).astype(F32) + 0.5) * (1.0 / channels)) for channel in range(own)]

    def finish(unit):
        @pl.when(unit < near)
        def _():
            for side in range(2):
                station = unit + side * near
                agreed = [full[unit, i, :, side * dirs : (side + 1) * dirs] for i in range(3)]
                for i in range(3):
                    consensus_out[i, station] = agreed[i]
                for channel in range(own):
                    smooth = sum(basis[channel][i] * agreed[i] for i in range(3))
                    duals_out[channel, station] = duals_ref[channel, station] + RHO_PENALTY * (
                        jones_ref[channel, station] - smooth
                    )

    finish(mine)
    for dx, dy in reversed(steps):
        finish(core * 16 + back(dx, dy))
    for n, c in enumerate(c5):
        c.wait_recv()
        dx, dy = ([(0, 0)] + list(reversed(steps)))[n]
        finish(other * 16 + back(dx, dy))
    for c in c1 + c2 + c3 + c4 + c5: c.wait_send()


def deliver_kernel(*refs):
    half = len(refs) // 2
    copies = [pltpu.make_async_copy(refs[n], refs[half + n], refs[-1].at[n]) for n in range(half)]
    for copy in copies:
        copy.start()
    for copy in copies:
        copy.wait()


def deliver(arrays):
    return pl.pallas_call(
        deliver_kernel,
        out_shape=tuple(jax.ShapeDtypeStruct(a.shape, a.dtype) for a in arrays),
        in_specs=[pl.BlockSpec(memory_space=pltpu.VMEM)] * len(arrays),
        out_specs=tuple(pl.BlockSpec(memory_space=pl.ANY) for _ in arrays),
        scratch_shapes=[pltpu.SemaphoreType.DMA((len(arrays),))],
        compiler_params=pltpu.CompilerParams(vmem_limit_bytes=2**20),
        name="deliver",
    )(*arrays)


def shards(jones_start, duals_start, consensus_start, visibilities, coherencies, pairs, counts):
    blocks = lax.axis_size("chan")
    channels = jones_start.shape[0] * lax.axis_size("grp") * blocks
    jones, duals, consensus = (jnp.transpose(a, (0, 3, 1, 2)) for a in (jones_start, duals_start, consensus_start))
    outs = descend(channels, blocks, pairs, counts, jones, duals, consensus, visibilities, coherencies)
    return tuple(jnp.transpose(a, (0, 2, 3, 1)) for a in deliver(outs))


def solution(mesh):
    in_specs = (
        P(("grp", "chan"), None, None, None),
        P(("grp", "chan"), None, None, None),
        P(),
        P(("grp", "chan"), None, None),
        P(("grp", "chan"), None, None, None),
        P(),
        P(("grp", "chan")),
    )
    out_specs = (P(("grp", "chan"), None, None, None), P(("grp", "chan"), None, None, None), P())
    return jax.shard_map(shards, mesh=mesh, in_specs=in_specs, out_specs=out_specs, check_vma=False)
```

```python
import functools

import jax
import jax.numpy as jnp
import numpy as np
from jax import lax
from jax.experimental import pallas as pl
from jax.experimental.pallas import tpu as pltpu
from jax.sharding import PartitionSpec as P

SAMPLES = 16
STEPS = 2
ETA_STEP = 0.08
RHO_PENALTY = 1.0
GROUP = 128
F32 = jnp.float32
BF16 = jnp.bfloat16
MESH = pl.DeviceIdType.MESH
SIDE = 4
FAR = 5


def bernstein(position):
    return [
        (1.0 - position) * (1.0 - position),
        2.0 * position * (1.0 - position),
        position * position,
    ]


def gram_inverse(channels):
    position = (np.arange(channels, dtype=np.float64) + 0.5) / channels
    values = np.stack(bernstein(position))
    matrix = values @ values.T
    rows = [np.cross(matrix[1], matrix[2]), np.cross(matrix[2], matrix[0]), np.cross(matrix[0], matrix[1])]
    return np.stack(rows).T / np.sum(matrix[0] * rows[0])


def triple(entry):
    return entry[0], entry[1] - entry[0], entry[0] + entry[1]


def total_of(values):
    return functools.reduce(lambda former, latter: former + latter, values)


def plain(factors):
    first = total_of([a[2] * b[0] for a, b in factors])
    return first - total_of([a[1] * b[2] for a, b in factors]), first + total_of([a[0] * b[1] for a, b in factors])


def conjugated(factors):
    return (
        total_of([a[2] * b[0] for a, b in factors]),
        total_of([a[1] * b[1] for a, b in factors]),
        total_of([a[0] * b[2] for a, b in factors]),
    )


def entries(values):
    return [(values[2 * n], values[2 * n + 1]) for n in range(4)]


def with_sum(entry):
    return entry[0], entry[1], entry[0] + entry[1]


def split(value):
    high = value.astype(BF16)
    low = (value - high.astype(F32)).astype(BF16)
    return high, low


def offsets():
    near = [min(n, SIDE - n) for n in range(SIDE)]
    pairs = [(dx, dy) for dx in range(SIDE) for dy in range(SIDE) if dx or dy]
    return sorted(pairs, key=lambda pair: -(near[pair[0]] + near[pair[1]]))


def greet(wait):
    barrier = pltpu.get_barrier_semaphore()
    z, chan = lax.axis_index("grp"), lax.axis_index("chan")
    core, u = chan % 2, chan // 2
    if wait:
        pl.semaphore_wait(barrier, 1 + SIDE * SIDE - 1 + SIDE - 1 + FAR)
        return
    pl.semaphore_signal(barrier, inc=1, device_id={"grp": z, "chan": u * 2 + 1 - core}, device_id_type=MESH)
    for n, (dx, dy) in enumerate(offsets()):
        there = ((u // SIDE + dx) % SIDE) * SIDE + (u % SIDE + dy) % SIDE
        for side in (core, 1 - core) if n < FAR else (core,):
            pl.semaphore_signal(
                barrier, inc=1, device_id={"grp": z, "chan": there * 2 + side}, device_id_type=MESH
            )
    for dz in range(1, SIDE):
        pl.semaphore_signal(barrier, inc=1, device_id={"grp": (z + dz) % SIDE, "chan": chan}, device_id_type=MESH)


def descend_kernel(
    channels, blocks, inverse, pairs_in, counts_ref, jones_in, duals_in, consensus_in, vis_in, coh_in,
    jones_out, duals_out, consensus_out, sums_out,
    pairs_pad, vis_pad, coh_tail, spread_hot, jones_cur, base, turned, both_now,
    propagated_now, turned_now, grad_parts, update_now, pairs_ref, jones_ref, duals_ref, consensus_ref, vis_ref, coh_ref,
    arrived, *links,
):
    own, stations, _, dirs = jones_ref.shape
    count = pairs_ref.shape[1]
    groups = spread_hot.shape[0]
    full = count // GROUP
    rows = 8 * dirs
    offset = (lax.axis_index("grp") * blocks + lax.axis_index("chan")) * own

    greet(False)
    inputs = [
        (pairs_in, pairs_ref), (jones_in, jones_ref), (vis_in, vis_ref), (consensus_in, consensus_ref),
        (duals_in, duals_ref),
    ]
    for channel in range(own):
        inputs.extend((coh_in.at[channel, c], coh_ref.at[channel, c]) for c in range(8))
    inputs = [pltpu.make_async_copy(a, b, arrived.at[n]) for n, (a, b) in enumerate(inputs)]
    for copy in inputs:
        copy.start()

    pairs_pad[...] = jnp.full(pairs_pad.shape, -1, jnp.int32)
    inputs[0].wait()
    pairs_pad[0:2, 0:count] = pairs_ref[...]

    ids = lax.broadcasted_iota(jnp.int32, (GROUP, GROUP), 0)
    for group in range(groups):
        for side in range(2):
            row = pairs_pad[side : side + 1, group * GROUP : (group + 1) * GROUP]
            hot = jnp.where(ids == row, 1.0, 0.0).astype(BF16)
            for part in range(2):
                where = (2 * side + part) * GROUP
                spread_hot[group, :, where : where + GROUP] = hot

    inputs[2].wait()
    vis_pad[...] = jnp.zeros(vis_pad.shape, F32)
    vis_pad[:, :, 0:count] = vis_ref[...]
    for copy in (inputs[1], inputs[3], inputs[4]):
        copy.wait()

    basis = []
    for channel in range(own):
        position = ((offset + channel).astype(F32) + 0.5) * (1.0 / channels)
        basis.append(bernstein(position))
        target = sum(basis[channel][i] * consensus_ref[i] for i in range(3))
        turned[channel] = ETA_STEP * (RHO_PENALTY * target - duals_ref[channel])
        base[channel] = jnp.zeros(base.shape[1:], F32)
        jones_cur[channel] = jnp.zeros(jones_cur.shape[1:], F32)
        for c in range(8):
            jones_cur[channel, c, :, 0:stations] = jones_ref[channel, :, c, :].T

    def turn(channel):
        for c in range(8):
            base[channel, c, :, 0:stations] = turned[channel, :, c, :].T

    def coherency(channel, group, comp, first):
        if isinstance(group, int) and group == full:
            return coh_tail[channel, comp, first : first + 16, :].astype(F32)
        lanes = pl.ds(pl.multiple_of(group * GROUP, GROUP), GROUP)
        return coh_ref[channel, comp, first : first + 16, lanes].astype(F32)

    def scatter_part(channel, group, side):
        lanes = slice(2 * side * GROUP, 2 * (side + 1) * GROUP)
        update_now[channel][...] += lax.dot_general(
            grad_parts[channel][:, lanes], spread_hot[group, :, lanes], (((1,), (1,)), ((), ())),
            preferred_element_type=F32,
        )

    def scatter(channel, group):
        for side in range(2):
            scatter_part(channel, group, side)

    def stations_of(side, group):
        lanes = pl.ds(group * GROUP if isinstance(group, int) else pl.multiple_of(group * GROUP, GROUP), GROUP)
        return jnp.broadcast_to(jnp.maximum(pairs_pad[side : side + 1, lanes], 0), (8, GROUP))

    def fetch(channel, which, first_row, depth):
        for row in range(first_row, first_row + depth, 8):
            for c in range(8):
                table = jones_cur[channel, c, row : row + 8, :]
                for side in range(2):
                    both_now[channel][c * dirs + row : c * dirs + row + 8, side * GROUP : (side + 1) * GROUP] = (
                        jnp.take_along_axis(table, which[side], axis=1)
                    )

    def visit(channel, group, factor, following=None, between=(None, None, None)):
        both, propagated_ref, turned_ref = both_now[channel], propagated_now[channel], turned_now[channel]
        parts = grad_parts[channel]
        lanes = pl.ds(group * GROUP if isinstance(group, int) else pl.multiple_of(group * GROUP, GROUP), GROUP)
        total = None
        for first_row in range(0, dirs, 16):
            wide = [coherency(channel, group, c, first_row) for c in range(8)]
            for upper in range(2):
                at = [slice(c * dirs + first_row + 8 * upper, c * dirs + first_row + 8 * upper + 8) for c in range(8)]
                source = [with_sum(e) for e in entries([w[8 * upper : 8 * upper + 8] for w in wide])]
                first = [triple(e) for e in entries([both[at[c], 0:GROUP] for c in range(8)])]
                propagated = []
                for row in range(2):
                    for col in range(2):
                        value = plain([(source[2 * m + col], first[2 * row + m]) for m in range(2)])
                        for part in range(2):
                            propagated_ref[at[2 * (2 * row + col) + part], :] = value[part]
                        propagated.append(with_sum(value))
                second = [triple(e) for e in entries([both[at[c], GROUP : 2 * GROUP] for c in range(8)])]
                model = []
                for row in range(2):
                    for col in range(2):
                        model.extend(conjugated([(propagated[2 * row + n], second[2 * col + n]) for n in range(2)]))
                total = model if total is None else [t + m for t, m in zip(total, model)]
                for row in range(2):
                    for col in range(2):
                        one, two, three = conjugated([(source[2 * col + n], second[2 * row + n]) for n in range(2)])
                        turned_ref[at[2 * (2 * row + col)], :] = one + two
                        turned_ref[at[2 * (2 * row + col) + 1], :] = three - one
        if between[0]:
            between[0]()
        lanes = pl.ds(pl.multiple_of(group * GROUP, GROUP), GROUP)
        residual = []
        for n in range(4):
            sums = [jnp.sum(total[3 * n + part], axis=0, keepdims=True) for part in range(3)]
            pair = (sums[0] + sums[1], sums[0] - sums[2])
            observed = [vis_pad[channel, 2 * n + part : 2 * n + part + 1, lanes] for part in range(2)]
            pair = triple([(observed[part] - pair[part]) * factor for part in range(2)])
            residual.append([jnp.broadcast_to(value, (16, GROUP)) for value in pair])
        place = [slice(n * GROUP, (n + 1) * GROUP) for n in range(4)]
        if following:
            which = [stations_of(side, following[1]) for side in range(2)]
        for first_row in range(0, dirs, 16):
            at = [slice(c * dirs + first_row, c * dirs + first_row + 16) for c in range(8)]
            turned_jones = [with_sum(e) for e in entries([turned_ref[at[c], :] for c in range(8)])]
            for row in range(2):
                for col in range(2):
                    value = plain([(turned_jones[2 * b + col], residual[2 * row + b]) for b in range(2)])
                    for part in range(2):
                        where = at[2 * (2 * row + col) + part]
                        parts[where, place[0]], parts[where, place[1]] = split(value[part])
            propagated = [with_sum(e) for e in entries([propagated_ref[at[c], :] for c in range(8)])]
            for row in range(2):
                for col in range(2):
                    one, two, three = conjugated([(propagated[2 * a + col], residual[2 * a + row]) for a in range(2)])
                    for part, value in enumerate((one + two, one - three)):
                        where = at[2 * (2 * row + col) + part]
                        parts[where, place[2]], parts[where, place[3]] = split(value)
            if following:
                fetch(following[0], which, first_row, 16)
            if between[1] and first_row == dirs // 2 - 16:
                between[1]()
        if between[2]:
            between[2]()

    for copy in inputs[5:]:
        copy.wait()
    coh_tail[...] = jnp.zeros(coh_tail.shape, BF16)
    coh_tail[:, :, :, 0 : count - full * GROUP] = coh_ref[:, :, :, full * GROUP : count]
    factors = [counts_ref[channel].astype(F32) * (2.0 * ETA_STEP / SAMPLES) for channel in range(own)]

    def step(_, carry):
        for channel in range(own):
            update_now[channel][...] = jnp.zeros((rows, GROUP), F32)
        grad_parts[1][...] = jnp.zeros(grad_parts[1].shape, BF16)

        fetch(0, [stations_of(side, 0) for side in range(2)], 0, dirs)

        def sweep(group, carry):
            before = jnp.maximum(group - 1, 0)
            visit(0, group, factors[0], (1, group), [
                None, None, lambda: scatter(1, before)
            ])
            visit(1, group, factors[1], (0, group + 1), [
                None, None, lambda: scatter(0, group)
            ])
            return carry

        lax.fori_loop(0, groups - 1, sweep, 0)
        last = groups - 1
        visit(0, last, factors[0], (1, last))
        scatter(1, last - 1)
        turn(0)
        visit(1, last, factors[1], None, [None, lambda: turn(1), None])
        scatter(0, last)
        scatter(1, last)
        for channel in range(own):
            update = update_now[channel][...].reshape(8, dirs, GROUP)
            jones_cur[channel] = (1.0 - ETA_STEP * RHO_PENALTY) * jones_cur[channel] + base[channel] + update
        return carry

    lax.fori_loop(0, STEPS, step, 0)

    for channel in range(own):
        for c in range(8):
            jones_out[channel, :, c, :] = jones_cur[channel, c].T[0:stations]
    near = stations // 2
    joined = [jones_out[channel] + duals_ref[channel] * (1.0 / RHO_PENALTY) for channel in range(own)]
    for i in range(3):
        value = sum(basis[channel][i] * joined[channel] for channel in range(own))
        sums_out[0:near, i] = jnp.concatenate([value[0:near], value[near : 2 * near]], axis=2)
        sums_out[near, i] = jnp.zeros((8, GROUP), F32)
    agree_kernel(channels, blocks, inverse, sums_out, jones_out, duals_ref, consensus_out, duals_out, *links)


def descend(channels, blocks, pairs, counts, jones, duals, consensus, visibilities, coherencies):
    own, stations, _, dirs = jones.shape
    count = pairs.shape[1]
    groups = -(-count // GROUP)
    lanes = groups * GROUP
    rows = 8 * dirs
    unit = (3, 8, GROUP)
    planes = SIDE * SIDE
    dma = pltpu.SemaphoreType.DMA
    inverse = [[float(v) for v in row] for row in gram_inverse(channels).astype(np.float32)]
    vmem = pl.BlockSpec(memory_space=pltpu.VMEM)
    smem = pl.BlockSpec(memory_space=pltpu.SMEM)
    anywhere = pl.BlockSpec(memory_space=pl.ANY)
    return pl.pallas_call(
        functools.partial(descend_kernel, channels, blocks, inverse),
        out_shape=tuple(pltpu.VMEM(a.shape, F32) for a in (jones, duals, consensus)),
        in_specs=[anywhere, smem] + [anywhere] * 5,
        out_specs=(vmem, vmem, vmem),
        scratch_shapes=[
            pltpu.VMEM((stations // 2 + 1,) + unit, F32),
            pltpu.VMEM((8, lanes), jnp.int32),
            pltpu.VMEM((own, 8, lanes), F32),
            pltpu.VMEM((own, 8, dirs, GROUP), BF16),
            pltpu.VMEM((groups, GROUP, 4 * GROUP), BF16),
            pltpu.VMEM((own, 8, dirs, GROUP), F32),
            pltpu.VMEM((own, 8, dirs, GROUP), F32),
            pltpu.VMEM((own, stations, 8, dirs), F32),
            [pltpu.VMEM((rows, 2 * GROUP), F32)] * own,
            [pltpu.VMEM((rows, GROUP), F32)] * own,
            [pltpu.VMEM((rows, GROUP), F32)] * own,
            [pltpu.VMEM((rows, 4 * GROUP), BF16)] * own,
            [pltpu.VMEM((rows, GROUP), F32)] * own,
        ]
        + [pltpu.VMEM(a.shape, a.dtype) for a in (pairs, jones, duals, consensus, visibilities, coherencies)]
        + [dma((5 + 8 * own,))]
        + [pltpu.VMEM((planes,) + unit, F32)] * 3
        + [pltpu.VMEM((FAR,) + unit, F32)]
        + [pltpu.VMEM((SIDE,) + unit, F32), pltpu.VMEM((2 * planes,) + unit, F32)]
        + [dma((planes,))] * 4
        + [dma((SIDE,))] * 2
        + [dma((planes,))] * 4
        + [dma((FAR,))] * 4,
        compiler_params=pltpu.CompilerParams(
            collective_id=0, has_side_effects=True, vmem_limit_bytes=56 * 2**20
        ),
        name="descend",
    )(pairs, counts, jones, duals, consensus, visibilities, coherencies)


def agree_kernel(
    channels, blocks, inverse, s_ref, jones_ref, duals_ref, consensus_out, duals_out,
    recv_core, mid, recv_plane, recv_far, recv_col, full, s1, r1, s2, r2, s3, r3, s4, r4, s5, r5, s6, r6, s7, r7,
):
    z = lax.axis_index("grp"); chan = lax.axis_index("chan")
    core = chan % 2; u = chan // 2; x = u // SIDE; y = u % SIDE
    other = 1 - core
    def peer(dx, dy):
        return ((x + dx) % SIDE) * SIDE + (y + dy) % SIDE
    steps = offsets()
    def back(dx, dy):
        return ((x - dx + SIDE) % SIDE) * SIDE + (y - dy + SIDE) % SIDE
    def dev(uu, cc): return {"grp": z, "chan": uu * 2 + cc}
    greet(True)
    order = steps + [(0, 0)]
    last = len(steps)

    def send(source, target, sent, received, device):
        copy = pltpu.make_async_remote_copy(
            src_ref=source, dst_ref=target, send_sem=sent, recv_sem=received, device_id=device, device_id_type=MESH
        )
        copy.start()
        return copy

    c2, c6 = {}, {}
    for n, (dx, dy) in enumerate(order[:FAR]):
        there = peer(dx, dy)
        c2[n] = send(s_ref.at[core * 16 + there], recv_plane.at[n], s2.at[n], r2.at[n], dev(there, core))
        c6[n] = send(s_ref.at[other * 16 + there], recv_far.at[n], s6.at[n], r6.at[n], dev(there, other))
    c1 = {}
    for n, (dx, dy) in enumerate(order):
        if n >= FAR:
            c1[n] = send(s_ref.at[other * 16 + peer(dx, dy)], recv_core.at[n], s1.at[n], r1.at[n], dev(u, other))
    for n, (dx, dy) in enumerate(order):
        if n >= FAR:
            c1[n].wait_recv()
            mid[n] = s_ref[core * 16 + peer(dx, dy)] + recv_core[n]
            if n < last:
                c2[n] = send(mid.at[n], recv_plane.at[n], s2.at[n], r2.at[n], dev(peer(dx, dy), core))
    total = mid[last]
    for n in reversed(range(last)):
        c2[n].wait_recv()
        total = total + recv_plane[n]
        if n < FAR:
            c6[n].wait_recv()
            total = total + recv_far[n]
    recv_col[z] = total
    c3 = [
        send(recv_col.at[z], recv_col.at[z], s3.at[dz], r3.at[dz], {"grp": (z + dz) % SIDE, "chan": chan})
        for dz in range(1, SIDE)
    ]
    for copy in c3:
        copy.wait_recv()
    total = recv_col[0] + recv_col[1] + recv_col[2] + recv_col[3]
    mine = core * 16 + u
    for i in range(3):
        full[mine, i] = sum(inverse[i][j] * total[j] for j in range(3))
    c4, c5, c7 = {}, {}, {}
    for n, (dx, dy) in enumerate(steps):
        there = peer(dx, dy)
        c4[n] = send(full.at[mine], full.at[mine], s4.at[n], r4.at[n], dev(there, core))
        if n < FAR:
            c7[n] = send(full.at[mine], full.at[mine], s7.at[n], r7.at[n], dev(there, other))
    c5[last] = send(full.at[mine], full.at[mine], s5.at[last], r5.at[last], dev(u, other))
    for n in reversed(range(last)):
        c4[n].wait_recv()
        if n >= FAR:
            unit = core * 16 + back(*steps[n])
            c5[n] = send(full.at[unit], full.at[unit], s5.at[n], r5.at[n], dev(u, other))
    own, stations, _, dirs = jones_ref.shape
    near = stations // 2
    offset = (z * blocks + chan) * own
    basis = [bernstein(((offset + channel).astype(F32) + 0.5) * (1.0 / channels)) for channel in range(own)]

    def finish(unit):
        @pl.when(unit < near)
        def _():
            for side in range(2):
                station = unit + side * near
                agreed = [full[unit, i, :, side * dirs : (side + 1) * dirs] for i in range(3)]
                for i in range(3):
                    consensus_out[i, station] = agreed[i]
                for channel in range(own):
                    smooth = sum(basis[channel][i] * agreed[i] for i in range(3))
                    duals_out[channel, station] = duals_ref[channel, station] + RHO_PENALTY * (
                        jones_ref[channel, station] - smooth
                    )

    finish(mine)
    for n in reversed(range(last)):
        finish(core * 16 + back(*steps[n]))
    for n in reversed(range(FAR, last + 1)):
        c5[n].wait_recv()
        finish(other * 16 + back(*order[n]))
    for n in range(FAR):
        c7[n].wait_recv()
        finish(other * 16 + back(*steps[n]))
    for copies in (c1, c2, c4, c5, c6, c7):
        for copy in copies.values():
            copy.wait_send()
    for copy in c3:
        copy.wait_send()


def deliver_kernel(*refs):
    half = len(refs) // 2
    copies = [pltpu.make_async_copy(refs[n], refs[half + n], refs[-1].at[n]) for n in range(half)]
    for copy in copies:
        copy.start()
    for copy in copies:
        copy.wait()


def deliver(arrays):
    return pl.pallas_call(
        deliver_kernel,
        out_shape=tuple(jax.ShapeDtypeStruct(a.shape, a.dtype) for a in arrays),
        in_specs=[pl.BlockSpec(memory_space=pltpu.VMEM)] * len(arrays),
        out_specs=tuple(pl.BlockSpec(memory_space=pl.ANY) for _ in arrays),
        scratch_shapes=[pltpu.SemaphoreType.DMA((len(arrays),))],
        compiler_params=pltpu.CompilerParams(vmem_limit_bytes=2**20),
        name="deliver",
    )(*arrays)


def shards(jones_start, duals_start, consensus_start, visibilities, coherencies, pairs, counts):
    blocks = lax.axis_size("chan")
    channels = jones_start.shape[0] * lax.axis_size("grp") * blocks
    jones, duals, consensus = (jnp.transpose(a, (0, 3, 1, 2)) for a in (jones_start, duals_start, consensus_start))
    outs = descend(channels, blocks, pairs, counts, jones, duals, consensus, visibilities, coherencies)
    return tuple(jnp.transpose(a, (0, 2, 3, 1)) for a in deliver(outs))


def solution(mesh):
    in_specs = (
        P(("grp", "chan"), None, None, None),
        P(("grp", "chan"), None, None, None),
        P(),
        P(("grp", "chan"), None, None),
        P(("grp", "chan"), None, None, None),
        P(),
        P(("grp", "chan")),
    )
    out_specs = (P(("grp", "chan"), None, None, None), P(("grp", "chan"), None, None, None), P())
    return jax.shard_map(shards, mesh=mesh, in_specs=in_specs, out_specs=out_specs, check_vma=False)
```

```python
import functools

import jax
import jax.numpy as jnp
import numpy as np
from jax import lax
from jax.experimental import pallas as pl
from jax.experimental.pallas import tpu as pltpu
from jax.sharding import PartitionSpec as P

SAMPLES = 16
STEPS = 2
ETA_STEP = 0.08
RHO_PENALTY = 1.0
GROUP = 128
F32 = jnp.float32
BF16 = jnp.bfloat16
MESH = pl.DeviceIdType.MESH
SIDE = 4


def bernstein(position):
    return [
        (1.0 - position) * (1.0 - position),
        2.0 * position * (1.0 - position),
        position * position,
    ]


def gram_inverse(channels):
    position = (np.arange(channels, dtype=np.float64) + 0.5) / channels
    values = np.stack(bernstein(position))
    matrix = values @ values.T
    rows = [np.cross(matrix[1], matrix[2]), np.cross(matrix[2], matrix[0]), np.cross(matrix[0], matrix[1])]
    return np.stack(rows).T / np.sum(matrix[0] * rows[0])


def triple(entry):
    return entry[0], entry[1] - entry[0], entry[0] + entry[1]


def total_of(values):
    return functools.reduce(lambda former, latter: former + latter, values)


def plain(factors):
    first = total_of([a[2] * b[0] for a, b in factors])
    return first - total_of([a[1] * b[2] for a, b in factors]), first + total_of([a[0] * b[1] for a, b in factors])


def conjugated(factors):
    return (
        total_of([a[2] * b[0] for a, b in factors]),
        total_of([a[1] * b[1] for a, b in factors]),
        total_of([a[0] * b[2] for a, b in factors]),
    )


def entries(values):
    return [(values[2 * n], values[2 * n + 1]) for n in range(4)]


def with_sum(entry):
    return entry[0], entry[1], entry[0] + entry[1]


def split(value):
    high = value.astype(BF16)
    low = (value - high.astype(F32)).astype(BF16)
    return high, low


def greet(wait):
    barrier = pltpu.get_barrier_semaphore()
    z, chan = lax.axis_index("grp"), lax.axis_index("chan")
    core, u = chan % 2, chan // 2
    if wait:
        pl.semaphore_wait(barrier, 1 + SIDE * SIDE - 1 + SIDE - 1)
        return
    pl.semaphore_signal(barrier, inc=1, device_id={"grp": z, "chan": u * 2 + 1 - core}, device_id_type=MESH)
    for dx in range(SIDE):
        for dy in range(SIDE):
            if dx or dy:
                there = ((u // SIDE + dx) % SIDE) * SIDE + (u % SIDE + dy) % SIDE
                pl.semaphore_signal(
                    barrier, inc=1, device_id={"grp": z, "chan": there * 2 + core}, device_id_type=MESH
                )
    for dz in range(1, SIDE):
        pl.semaphore_signal(barrier, inc=1, device_id={"grp": (z + dz) % SIDE, "chan": chan}, device_id_type=MESH)


def descend_kernel(
    channels, blocks, inverse, pairs_in, counts_ref, jones_in, duals_in, consensus_in, vis_in, coh_in,
    jones_out, duals_out, consensus_out, sums_out,
    pairs_pad, vis_pad, coh_tail, spread_hot, jones_cur, base, turned, both_now,
    propagated_now, turned_now, grad_parts, update_now, pairs_ref, jones_ref, duals_ref, consensus_ref, vis_ref, coh_ref,
    arrived, *links,
):
    own, stations, _, dirs = jones_ref.shape
    count = pairs_ref.shape[1]
    groups = spread_hot.shape[0]
    full = count // GROUP
    rows = 8 * dirs
    offset = (lax.axis_index("grp") * blocks + lax.axis_index("chan")) * own

    greet(False)
    inputs = [
        (pairs_in, pairs_ref), (jones_in, jones_ref), (vis_in, vis_ref), (consensus_in, consensus_ref),
        (duals_in, duals_ref),
    ]
    for channel in range(own):
        inputs.extend((coh_in.at[channel, c], coh_ref.at[channel, c]) for c in range(8))
    inputs = [pltpu.make_async_copy(a, b, arrived.at[n]) for n, (a, b) in enumerate(inputs)]
    for copy in inputs:
        copy.start()

    pairs_pad[...] = jnp.full(pairs_pad.shape, -1, jnp.int32)
    inputs[0].wait()
    pairs_pad[0:2, 0:count] = pairs_ref[...]

    ids = lax.broadcasted_iota(jnp.int32, (GROUP, GROUP), 0)
    for group in range(groups):
        for side in range(2):
            row = pairs_pad[side : side + 1, group * GROUP : (group + 1) * GROUP]
            hot = jnp.where(ids == row, 1.0, 0.0).astype(BF16)
            for part in range(2):
                where = (2 * side + part) * GROUP
                spread_hot[group, :, where : where + GROUP] = hot

    inputs[2].wait()
    vis_pad[...] = jnp.zeros(vis_pad.shape, F32)
    vis_pad[:, :, 0:count] = vis_ref[...]
    for copy in (inputs[1], inputs[3], inputs[4]):
        copy.wait()

    basis = []
    for channel in range(own):
        position = ((offset + channel).astype(F32) + 0.5) * (1.0 / channels)
        basis.append(bernstein(position))
        target = sum(basis[channel][i] * consensus_ref[i] for i in range(3))
        turned[channel] = ETA_STEP * (RHO_PENALTY * target - duals_ref[channel])
        base[channel] = jnp.zeros(base.shape[1:], F32)
        jones_cur[channel] = jnp.zeros(jones_cur.shape[1:], F32)
        for c in range(8):
            jones_cur[channel, c, :, 0:stations] = jones_ref[channel, :, c, :].T

    def turn(channel):
        for c in range(8):
            base[channel, c, :, 0:stations] = turned[channel, :, c, :].T

    def coherency(channel, group, comp, first):
        if isinstance(group, int) and group == full:
            return coh_tail[channel, comp, first : first + 16, :].astype(F32)
        lanes = pl.ds(pl.multiple_of(group * GROUP, GROUP), GROUP)
        return coh_ref[channel, comp, first : first + 16, lanes].astype(F32)

    def scatter_part(channel, group, side):
        lanes = slice(2 * side * GROUP, 2 * (side + 1) * GROUP)
        update_now[channel][...] += lax.dot_general(
            grad_parts[channel][:, lanes], spread_hot[group, :, lanes], (((1,), (1,)), ((), ())),
            preferred_element_type=F32,
        )

    def scatter(channel, group):
        for side in range(2):
            scatter_part(channel, group, side)

    def stations_of(side, group):
        lanes = pl.ds(group * GROUP if isinstance(group, int) else pl.multiple_of(group * GROUP, GROUP), GROUP)
        return jnp.broadcast_to(jnp.maximum(pairs_pad[side : side + 1, lanes], 0), (8, GROUP))

    def fetch(channel, which, first_row, depth, sides=(0, 1)):
        for row in range(first_row, first_row + depth, 8):
            for c in range(8):
                table = jones_cur[channel, c, row : row + 8, :]
                for side in sides:
                    both_now[channel][c * dirs + row : c * dirs + row + 8, side * GROUP : (side + 1) * GROUP] = (
                        jnp.take_along_axis(table, which[side], axis=1)
                    )

    def visit(channel, group, factor, following=None, between=(None, None, None)):
        both, propagated_ref, turned_ref = both_now[channel], propagated_now[channel], turned_now[channel]
        parts = grad_parts[channel]
        lanes = pl.ds(group * GROUP if isinstance(group, int) else pl.multiple_of(group * GROUP, GROUP), GROUP)
        total = None
        if following:
            which = [stations_of(side, following[1]) for side in range(2)]
        for first_row in range(0, dirs, 16):
            if following and first_row < 32:
                fetch(following[0], which, first_row, 16, (0,))
            wide = [coherency(channel, group, c, first_row) for c in range(8)]
            for upper in range(2):
                at = [slice(c * dirs + first_row + 8 * upper, c * dirs + first_row + 8 * upper + 8) for c in range(8)]
                source = [with_sum(e) for e in entries([w[8 * upper : 8 * upper + 8] for w in wide])]
                first = [triple(e) for e in entries([both[at[c], 0:GROUP] for c in range(8)])]
                propagated = []
                for row in range(2):
                    for col in range(2):
                        value = plain([(source[2 * m + col], first[2 * row + m]) for m in range(2)])
                        for part in range(2):
                            propagated_ref[at[2 * (2 * row + col) + part], :] = value[part]
                        propagated.append(with_sum(value))
                second = [triple(e) for e in entries([both[at[c], GROUP : 2 * GROUP] for c in range(8)])]
                model = []
                for row in range(2):
                    for col in range(2):
                        model.extend(conjugated([(propagated[2 * row + n], second[2 * col + n]) for n in range(2)]))
                total = model if total is None else [t + m for t, m in zip(total, model)]
                for row in range(2):
                    for col in range(2):
                        one, two, three = conjugated([(source[2 * col + n], second[2 * row + n]) for n in range(2)])
                        turned_ref[at[2 * (2 * row + col)], :] = one + two
                        turned_ref[at[2 * (2 * row + col) + 1], :] = three - one
        if between[0]:
            between[0]()
        lanes = pl.ds(pl.multiple_of(group * GROUP, GROUP), GROUP)
        residual = []
        for n in range(4):
            sums = [jnp.sum(total[3 * n + part], axis=0, keepdims=True) for part in range(3)]
            pair = (sums[0] + sums[1], sums[0] - sums[2])
            observed = [vis_pad[channel, 2 * n + part : 2 * n + part + 1, lanes] for part in range(2)]
            pair = triple([(observed[part] - pair[part]) * factor for part in range(2)])
            residual.append([jnp.broadcast_to(value, (16, GROUP)) for value in pair])
        place = [slice(n * GROUP, (n + 1) * GROUP) for n in range(4)]
        if following:
            which = [stations_of(side, following[1]) for side in range(2)]
        for first_row in range(0, dirs, 16):
            at = [slice(c * dirs + first_row, c * dirs + first_row + 16) for c in range(8)]
            turned_jones = [with_sum(e) for e in entries([turned_ref[at[c], :] for c in range(8)])]
            for row in range(2):
                for col in range(2):
                    value = plain([(turned_jones[2 * b + col], residual[2 * row + b]) for b in range(2)])
                    for part in range(2):
                        where = at[2 * (2 * row + col) + part]
                        parts[where, place[0]], parts[where, place[1]] = split(value[part])
            propagated = [with_sum(e) for e in entries([propagated_ref[at[c], :] for c in range(8)])]
            for row in range(2):
                for col in range(2):
                    one, two, three = conjugated([(propagated[2 * a + col], residual[2 * a + row]) for a in range(2)])
                    for part, value in enumerate((one + two, one - three)):
                        where = at[2 * (2 * row + col) + part]
                        parts[where, place[2]], parts[where, place[3]] = split(value)
            if following:
                fetch(following[0], which, first_row, 16, (0, 1) if first_row >= 32 else (1,))
            if between[1] and first_row == dirs // 2 - 16:
                between[1]()
        if between[2]:
            between[2]()

    for copy in inputs[5:]:
        copy.wait()
    coh_tail[...] = jnp.zeros(coh_tail.shape, BF16)
    coh_tail[:, :, :, 0 : count - full * GROUP] = coh_ref[:, :, :, full * GROUP : count]
    factors = [counts_ref[channel].astype(F32) * (2.0 * ETA_STEP / SAMPLES) for channel in range(own)]

    def step(_, carry):
        for channel in range(own):
            update_now[channel][...] = jnp.zeros((rows, GROUP), F32)
        grad_parts[1][...] = jnp.zeros(grad_parts[1].shape, BF16)

        fetch(0, [stations_of(side, 0) for side in range(2)], 0, dirs)

        def sweep(group, carry):
            before = jnp.maximum(group - 1, 0)
            visit(0, group, factors[0], (1, group), [
                None, None, lambda: scatter(1, before)
            ])
            visit(1, group, factors[1], (0, group + 1), [
                None, None, lambda: scatter(0, group)
            ])
            return carry

        lax.fori_loop(0, groups - 1, sweep, 0)
        last = groups - 1
        visit(0, last, factors[0], (1, last))
        scatter(1, last - 1)
        turn(0)
        visit(1, last, factors[1], None, [None, lambda: turn(1), None])
        scatter(0, last)
        scatter(1, last)
        for channel in range(own):
            update = update_now[channel][...].reshape(8, dirs, GROUP)
            jones_cur[channel] = (1.0 - ETA_STEP * RHO_PENALTY) * jones_cur[channel] + base[channel] + update
        return carry

    lax.fori_loop(0, STEPS, step, 0)

    for channel in range(own):
        for c in range(8):
            jones_out[channel, :, c, :] = jones_cur[channel, c].T[0:stations]
    near = stations // 2
    joined = [jones_out[channel] + duals_ref[channel] * (1.0 / RHO_PENALTY) for channel in range(own)]
    for i in range(3):
        value = sum(basis[channel][i] * joined[channel] for channel in range(own))
        sums_out[0:near, i] = jnp.concatenate([value[0:near], value[near : 2 * near]], axis=2)
        sums_out[near, i] = jnp.zeros((8, GROUP), F32)
    agree_kernel(channels, blocks, inverse, sums_out, jones_out, duals_ref, consensus_out, duals_out, *links)


def descend(channels, blocks, pairs, counts, jones, duals, consensus, visibilities, coherencies):
    own, stations, _, dirs = jones.shape
    count = pairs.shape[1]
    groups = -(-count // GROUP)
    lanes = groups * GROUP
    rows = 8 * dirs
    unit = (3, 8, GROUP)
    planes = SIDE * SIDE
    dma = pltpu.SemaphoreType.DMA
    inverse = [[float(v) for v in row] for row in gram_inverse(channels).astype(np.float32)]
    vmem = pl.BlockSpec(memory_space=pltpu.VMEM)
    smem = pl.BlockSpec(memory_space=pltpu.SMEM)
    anywhere = pl.BlockSpec(memory_space=pl.ANY)
    return pl.pallas_call(
        functools.partial(descend_kernel, channels, blocks, inverse),
        out_shape=tuple(pltpu.VMEM(a.shape, F32) for a in (jones, duals, consensus)),
        in_specs=[anywhere, smem] + [anywhere] * 5,
        out_specs=(vmem, vmem, vmem),
        scratch_shapes=[
            pltpu.VMEM((stations // 2 + 1,) + unit, F32),
            pltpu.VMEM((8, lanes), jnp.int32),
            pltpu.VMEM((own, 8, lanes), F32),
            pltpu.VMEM((own, 8, dirs, GROUP), BF16),
            pltpu.VMEM((groups, GROUP, 4 * GROUP), BF16),
            pltpu.VMEM((own, 8, dirs, GROUP), F32),
            pltpu.VMEM((own, 8, dirs, GROUP), F32),
            pltpu.VMEM((own, stations, 8, dirs), F32),
            [pltpu.VMEM((rows, 2 * GROUP), F32)] * own,
            [pltpu.VMEM((rows, GROUP), F32)] * own,
            [pltpu.VMEM((rows, GROUP), F32)] * own,
            [pltpu.VMEM((rows, 4 * GROUP), BF16)] * own,
            [pltpu.VMEM((rows, GROUP), F32)] * own,
        ]
        + [pltpu.VMEM(a.shape, a.dtype) for a in (pairs, jones, duals, consensus, visibilities, coherencies)]
        + [dma((5 + 8 * own,))]
        + [pltpu.VMEM((planes,) + unit, F32)] * 3
        + [pltpu.VMEM((SIDE,) + unit, F32), pltpu.VMEM((2 * planes,) + unit, F32)]
        + [dma((planes,))] * 4
        + [dma((SIDE,))] * 2
        + [dma((planes,))] * 4,
        compiler_params=pltpu.CompilerParams(
            collective_id=0, has_side_effects=True, vmem_limit_bytes=56 * 2**20
        ),
        name="descend",
    )(pairs, counts, jones, duals, consensus, visibilities, coherencies)


def agree_kernel(
    channels, blocks, inverse, s_ref, jones_ref, duals_ref, consensus_out, duals_out,
    recv_core, mid, recv_plane, recv_col, full, s1, r1, s2, r2, s3, r3, s4, r4, s5, r5,
):
    z = lax.axis_index("grp"); chan = lax.axis_index("chan")
    core = chan % 2; u = chan // 2; x = u // SIDE; y = u % SIDE
    other = 1 - core
    def peer(dx, dy):
        return ((x + dx) % SIDE) * SIDE + (y + dy) % SIDE
    steps = sorted([(dx, dy) for dx in range(SIDE) for dy in range(SIDE) if dx or dy], key=lambda s: -(min(s[0],4-s[0])+min(s[1],4-s[1])))
    def back(dx, dy):
        return ((x - dx + SIDE) % SIDE) * SIDE + (y - dy + SIDE) % SIDE
    def dev(uu, cc): return {"grp": z, "chan": uu * 2 + cc}
    greet(True)
    order = steps + [(0, 0)]
    def rc(src, dst, ss, rs, d):
        return pltpu.make_async_remote_copy(src_ref=src, dst_ref=dst, send_sem=ss, recv_sem=rs, device_id=d, device_id_type=MESH)
    c1 = []
    for n, (dx, dy) in enumerate(order):
        c = rc(s_ref.at[other * 16 + peer(dx, dy)], recv_core.at[n], s1.at[n], r1.at[n], dev(u, other))
        c.start(); c1.append(c)
    c2 = []
    for n, (dx, dy) in enumerate(order):
        c1[n].wait_recv()
        mid[n] = s_ref[core * 16 + peer(dx, dy)] + recv_core[n]
        if n < 15:
            c = rc(mid.at[n], recv_plane.at[n], s2.at[n], r2.at[n], dev(peer(dx, dy), core))
            c.start(); c2.append(c)
    total = mid[15]
    for n in range(15):
        c2[n].wait_recv()
        total = total + recv_plane[n]
    recv_col[z] = total
    c3 = []
    for dz in range(1, SIDE):
        c = rc(recv_col.at[z], recv_col.at[z], s3.at[dz], r3.at[dz], {"grp": (z + dz) % SIDE, "chan": chan})
        c.start(); c3.append(c)
    for c in c3: c.wait_recv()
    total = recv_col[0] + recv_col[1] + recv_col[2] + recv_col[3]
    mine = core * 16 + u
    for i in range(3):
        full[mine, i] = sum(inverse[i][j] * total[j] for j in range(3))
    c4 = []
    for n, (dx, dy) in enumerate(steps):
        c = rc(full.at[mine], full.at[mine], s4.at[n], r4.at[n], dev(peer(dx, dy), core))
        c.start(); c4.append(c)
    c5 = []
    c = rc(full.at[mine], full.at[mine], s5.at[15], r5.at[15], dev(u, other))
    c.start(); c5.append(c)
    for n, (dx, dy) in reversed(list(enumerate(steps))):
        c4[n].wait_recv()
        unit = core * 16 + back(dx, dy)
        c = rc(full.at[unit], full.at[unit], s5.at[n], r5.at[n], dev(u, other))
        c.start(); c5.append(c)
    own, stations, _, dirs = jones_ref.shape
    near = stations // 2
    offset = (z * blocks + chan) * own
    basis = [bernstein(((offset + channel).astype(F32) + 0.5) * (1.0 / channels)) for channel in range(own)]

    def finish(unit):
        @pl.when(unit < near)
        def _():
            for side in range(2):
                station = unit + side * near
                agreed = [full[unit, i, :, side * dirs : (side + 1) * dirs] for i in range(3)]
                for i in range(3):
                    consensus_out[i, station] = agreed[i]
                for channel in range(own):
                    smooth = sum(basis[channel][i] * agreed[i] for i in range(3))
                    duals_out[channel, station] = duals_ref[channel, station] + RHO_PENALTY * (
                        jones_ref[channel, station] - smooth
                    )

    finish(mine)
    for dx, dy in reversed(steps):
        finish(core * 16 + back(dx, dy))
    for n, c in enumerate(c5):
        c.wait_recv()
        dx, dy = ([(0, 0)] + list(reversed(steps)))[n]
        finish(other * 16 + back(dx, dy))
    for c in c1 + c2 + c3 + c4 + c5: c.wait_send()


def deliver_kernel(*refs):
    half = len(refs) // 2
    copies = [pltpu.make_async_copy(refs[n], refs[half + n], refs[-1].at[n]) for n in range(half)]
    for copy in copies:
        copy.start()
    for copy in copies:
        copy.wait()


def deliver(arrays):
    return pl.pallas_call(
        deliver_kernel,
        out_shape=tuple(jax.ShapeDtypeStruct(a.shape, a.dtype) for a in arrays),
        in_specs=[pl.BlockSpec(memory_space=pltpu.VMEM)] * len(arrays),
        out_specs=tuple(pl.BlockSpec(memory_space=pl.ANY) for _ in arrays),
        scratch_shapes=[pltpu.SemaphoreType.DMA((len(arrays),))],
        compiler_params=pltpu.CompilerParams(vmem_limit_bytes=2**20),
        name="deliver",
    )(*arrays)


def shards(jones_start, duals_start, consensus_start, visibilities, coherencies, pairs, counts):
    blocks = lax.axis_size("chan")
    channels = jones_start.shape[0] * lax.axis_size("grp") * blocks
    jones, duals, consensus = (jnp.transpose(a, (0, 3, 1, 2)) for a in (jones_start, duals_start, consensus_start))
    outs = descend(channels, blocks, pairs, counts, jones, duals, consensus, visibilities, coherencies)
    return tuple(jnp.transpose(a, (0, 2, 3, 1)) for a in deliver(outs))


def solution(mesh):
    in_specs = (
        P(("grp", "chan"), None, None, None),
        P(("grp", "chan"), None, None, None),
        P(),
        P(("grp", "chan"), None, None),
        P(("grp", "chan"), None, None, None),
        P(),
        P(("grp", "chan")),
    )
    out_specs = (P(("grp", "chan"), None, None, None), P(("grp", "chan"), None, None, None), P())
    return jax.shard_map(shards, mesh=mesh, in_specs=in_specs, out_specs=out_specs, check_vma=False)
```

```python
import functools

import jax
import jax.numpy as jnp
import numpy as np
from jax import lax
from jax.experimental import pallas as pl
from jax.experimental.pallas import tpu as pltpu
from jax.sharding import PartitionSpec as P

SAMPLES = 16
STEPS = 2
ETA_STEP = 0.08
RHO_PENALTY = 1.0
GROUP = 128
F32 = jnp.float32
BF16 = jnp.bfloat16
MESH = pl.DeviceIdType.MESH
SIDE = 4


def bernstein(position):
    return [
        (1.0 - position) * (1.0 - position),
        2.0 * position * (1.0 - position),
        position * position,
    ]


def gram_inverse(channels):
    position = (np.arange(channels, dtype=np.float64) + 0.5) / channels
    values = np.stack(bernstein(position))
    matrix = values @ values.T
    rows = [np.cross(matrix[1], matrix[2]), np.cross(matrix[2], matrix[0]), np.cross(matrix[0], matrix[1])]
    return np.stack(rows).T / np.sum(matrix[0] * rows[0])


def triple(entry):
    return entry[0], entry[1] - entry[0], entry[0] + entry[1]


def total_of(values):
    return functools.reduce(lambda former, latter: former + latter, values)


def plain(factors):
    first = total_of([a[2] * b[0] for a, b in factors])
    return first - total_of([a[1] * b[2] for a, b in factors]), first + total_of([a[0] * b[1] for a, b in factors])


def conjugated(factors):
    return (
        total_of([a[2] * b[0] for a, b in factors]),
        total_of([a[1] * b[1] for a, b in factors]),
        total_of([a[0] * b[2] for a, b in factors]),
    )


def entries(values):
    return [(values[2 * n], values[2 * n + 1]) for n in range(4)]


def with_sum(entry):
    return entry[0], entry[1], entry[0] + entry[1]


def split(value):
    high = value.astype(BF16)
    low = (value - high.astype(F32)).astype(BF16)
    return high, low


def greet(wait):
    barrier = pltpu.get_barrier_semaphore()
    z, chan = lax.axis_index("grp"), lax.axis_index("chan")
    core, u = chan % 2, chan // 2
    if wait:
        pl.semaphore_wait(barrier, 1 + SIDE * SIDE - 1 + SIDE - 1)
        return
    pl.semaphore_signal(barrier, inc=1, device_id={"grp": z, "chan": u * 2 + 1 - core}, device_id_type=MESH)
    for dx in range(SIDE):
        for dy in range(SIDE):
            if dx or dy:
                there = ((u // SIDE + dx) % SIDE) * SIDE + (u % SIDE + dy) % SIDE
                pl.semaphore_signal(
                    barrier, inc=1, device_id={"grp": z, "chan": there * 2 + core}, device_id_type=MESH
                )
    for dz in range(1, SIDE):
        pl.semaphore_signal(barrier, inc=1, device_id={"grp": (z + dz) % SIDE, "chan": chan}, device_id_type=MESH)


def descend_kernel(
    channels, blocks, inverse, pairs_in, counts_ref, jones_in, duals_in, consensus_in, vis_in, coh_in,
    jones_out, duals_out, consensus_out, sums_out,
    pairs_pad, vis_pad, coh_tail, spread_hot, jones_cur, base, turned, both_now,
    propagated_now, turned_now, grad_parts, update_now, pairs_ref, jones_ref, duals_ref, consensus_ref, vis_ref, coh_ref,
    arrived, *links,
):
    own, stations, _, dirs = jones_ref.shape
    count = pairs_ref.shape[1]
    groups = spread_hot.shape[0]
    full = count // GROUP
    rows = 8 * dirs
    offset = (lax.axis_index("grp") * blocks + lax.axis_index("chan")) * own

    greet(False)
    inputs = [
        (pairs_in, pairs_ref), (jones_in, jones_ref), (vis_in, vis_ref), (consensus_in, consensus_ref),
        (duals_in, duals_ref),
    ]
    for channel in range(own):
        inputs.extend((coh_in.at[channel, c], coh_ref.at[channel, c]) for c in range(8))
    inputs = [pltpu.make_async_copy(a, b, arrived.at[n]) for n, (a, b) in enumerate(inputs)]
    for copy in inputs:
        copy.start()

    pairs_pad[...] = jnp.full(pairs_pad.shape, -1, jnp.int32)
    inputs[0].wait()
    pairs_pad[0:2, 0:count] = pairs_ref[...]

    ids = lax.broadcasted_iota(jnp.int32, (GROUP, GROUP), 0)
    for group in range(groups):
        for side in range(2):
            row = pairs_pad[side : side + 1, group * GROUP : (group + 1) * GROUP]
            hot = jnp.where(ids == row, 1.0, 0.0).astype(BF16)
            for part in range(2):
                where = (2 * side + part) * GROUP
                spread_hot[group, :, where : where + GROUP] = hot

    inputs[2].wait()
    vis_pad[...] = jnp.zeros(vis_pad.shape, F32)
    vis_pad[:, :, 0:count] = vis_ref[...]
    for copy in (inputs[1], inputs[3], inputs[4]):
        copy.wait()

    basis = []
    for channel in range(own):
        position = ((offset + channel).astype(F32) + 0.5) * (1.0 / channels)
        basis.append(bernstein(position))
        target = sum(basis[channel][i] * consensus_ref[i] for i in range(3))
        turned[channel] = ETA_STEP * (RHO_PENALTY * target - duals_ref[channel])
        base[channel] = jnp.zeros(base.shape[1:], F32)
        jones_cur[channel] = jnp.zeros(jones_cur.shape[1:], F32)
        for c in range(8):
            jones_cur[channel, c, :, 0:stations] = jones_ref[channel, :, c, :].T

    def turn(channel):
        for c in range(8):
            base[channel, c, :, 0:stations] = turned[channel, :, c, :].T

    def coherency(channel, group, comp, first):
        if isinstance(group, int) and group == full:
            return coh_tail[channel, comp, first : first + 16, :].astype(F32)
        lanes = pl.ds(pl.multiple_of(group * GROUP, GROUP), GROUP)
        return coh_ref[channel, comp, first : first + 16, lanes].astype(F32)

    def scatter_part(channel, group, side):
        lanes = slice(2 * side * GROUP, 2 * (side + 1) * GROUP)
        update_now[channel][...] += lax.dot_general(
            grad_parts[channel][:, lanes], spread_hot[group, :, lanes], (((1,), (1,)), ((), ())),
            preferred_element_type=F32,
        )

    def scatter(channel, group):
        for side in range(2):
            scatter_part(channel, group, side)

    def stations_of(side, group):
        lanes = pl.ds(group * GROUP if isinstance(group, int) else pl.multiple_of(group * GROUP, GROUP), GROUP)
        return jnp.broadcast_to(jnp.maximum(pairs_pad[side : side + 1, lanes], 0), (8, GROUP))

    def fetch(channel, which, first_row, depth, sides=(0, 1)):
        for row in range(first_row, first_row + depth, 8):
            for c in range(8):
                table = jones_cur[channel, c, row : row + 8, :]
                for side in sides:
                    both_now[channel][c * dirs + row : c * dirs + row + 8, side * GROUP : (side + 1) * GROUP] = (
                        jnp.take_along_axis(table, which[side], axis=1)
                    )

    def visit(channel, group, factor, following=None, between=(None, None, None)):
        both, propagated_ref, turned_ref = both_now[channel], propagated_now[channel], turned_now[channel]
        parts = grad_parts[channel]
        lanes = pl.ds(group * GROUP if isinstance(group, int) else pl.multiple_of(group * GROUP, GROUP), GROUP)
        total = None
        if following:
            which = [stations_of(side, following[1]) for side in range(2)]
        for first_row in range(0, dirs, 16):
            if following and first_row < 32:
                fetch(following[0], which, first_row, 16, (0,))
            wide = [coherency(channel, group, c, first_row) for c in range(8)]
            for upper in range(2):
                at = [slice(c * dirs + first_row + 8 * upper, c * dirs + first_row + 8 * upper + 8) for c in range(8)]
                source = [with_sum(e) for e in entries([w[8 * upper : 8 * upper + 8] for w in wide])]
                first = [triple(e) for e in entries([both[at[c], 0:GROUP] for c in range(8)])]
                propagated = []
                for row in range(2):
                    for col in range(2):
                        value = plain([(source[2 * m + col], first[2 * row + m]) for m in range(2)])
                        for part in range(2):
                            propagated_ref[at[2 * (2 * row + col) + part], :] = value[part]
                        propagated.append(with_sum(value))
                second = [triple(e) for e in entries([both[at[c], GROUP : 2 * GROUP] for c in range(8)])]
                model = []
                for row in range(2):
                    for col in range(2):
                        model.extend(conjugated([(propagated[2 * row + n], second[2 * col + n]) for n in range(2)]))
                total = model if total is None else [t + m for t, m in zip(total, model)]
                for row in range(2):
                    for col in range(2):
                        one, two, three = conjugated([(source[2 * col + n], second[2 * row + n]) for n in range(2)])
                        turned_ref[at[2 * (2 * row + col)], :] = one + two
                        turned_ref[at[2 * (2 * row + col) + 1], :] = three - one
        if between[0]:
            between[0]()
        lanes = pl.ds(pl.multiple_of(group * GROUP, GROUP), GROUP)
        residual = []
        for n in range(4):
            sums = [jnp.sum(total[3 * n + part], axis=0, keepdims=True) for part in range(3)]
            pair = (sums[0] + sums[1], sums[0] - sums[2])
            observed = [vis_pad[channel, 2 * n + part : 2 * n + part + 1, lanes] for part in range(2)]
            pair = triple([(observed[part] - pair[part]) * factor for part in range(2)])
            residual.append([jnp.broadcast_to(value, (16, GROUP)) for value in pair])
        place = [slice(n * GROUP, (n + 1) * GROUP) for n in range(4)]
        if following:
            which = [stations_of(side, following[1]) for side in range(2)]
        for first_row in range(0, dirs, 16):
            at = [slice(c * dirs + first_row, c * dirs + first_row + 16) for c in range(8)]
            if following:
                fetch(following[0], which, first_row, 16, (0, 1) if first_row >= 32 else (1,))
            turned_jones = [with_sum(e) for e in entries([turned_ref[at[c], :] for c in range(8)])]
            for row in range(2):
                for col in range(2):
                    value = plain([(turned_jones[2 * b + col], residual[2 * row + b]) for b in range(2)])
                    for part in range(2):
                        where = at[2 * (2 * row + col) + part]
                        parts[where, place[0]], parts[where, place[1]] = split(value[part])
            propagated = [with_sum(e) for e in entries([propagated_ref[at[c], :] for c in range(8)])]
            for row in range(2):
                for col in range(2):
                    one, two, three = conjugated([(propagated[2 * a + col], residual[2 * a + row]) for a in range(2)])
                    for part, value in enumerate((one + two, one - three)):
                        where = at[2 * (2 * row + col) + part]
                        parts[where, place[2]], parts[where, place[3]] = split(value)
            if between[1] and first_row == dirs // 2 - 16:
                between[1]()
        if between[2]:
            between[2]()

    for copy in inputs[5:]:
        copy.wait()
    coh_tail[...] = jnp.zeros(coh_tail.shape, BF16)
    coh_tail[:, :, :, 0 : count - full * GROUP] = coh_ref[:, :, :, full * GROUP : count]
    factors = [counts_ref[channel].astype(F32) * (2.0 * ETA_STEP / SAMPLES) for channel in range(own)]

    def step(_, carry):
        for channel in range(own):
            update_now[channel][...] = jnp.zeros((rows, GROUP), F32)
        grad_parts[1][...] = jnp.zeros(grad_parts[1].shape, BF16)

        fetch(0, [stations_of(side, 0) for side in range(2)], 0, dirs)

        def sweep(group, carry):
            before = jnp.maximum(group - 1, 0)
            visit(0, group, factors[0], (1, group), [
                None, None, lambda: scatter(1, before)
            ])
            visit(1, group, factors[1], (0, group + 1), [
                None, None, lambda: scatter(0, group)
            ])
            return carry

        lax.fori_loop(0, groups - 1, sweep, 0)
        last = groups - 1
        visit(0, last, factors[0], (1, last))
        scatter(1, last - 1)
        turn(0)
        visit(1, last, factors[1], None, [None, lambda: turn(1), None])
        scatter(0, last)
        scatter(1, last)
        for channel in range(own):
            update = update_now[channel][...].reshape(8, dirs, GROUP)
            jones_cur[channel] = (1.0 - ETA_STEP * RHO_PENALTY) * jones_cur[channel] + base[channel] + update
        return carry

    lax.fori_loop(0, STEPS, step, 0)

    for channel in range(own):
        for c in range(8):
            jones_out[channel, :, c, :] = jones_cur[channel, c].T[0:stations]
    near = stations // 2
    joined = [jones_out[channel] + duals_ref[channel] * (1.0 / RHO_PENALTY) for channel in range(own)]
    for i in range(3):
        value = sum(basis[channel][i] * joined[channel] for channel in range(own))
        sums_out[0:near, i] = jnp.concatenate([value[0:near], value[near : 2 * near]], axis=2)
        sums_out[near, i] = jnp.zeros((8, GROUP), F32)
    agree_kernel(channels, blocks, inverse, sums_out, jones_out, duals_ref, consensus_out, duals_out, *links)


def descend(channels, blocks, pairs, counts, jones, duals, consensus, visibilities, coherencies):
    own, stations, _, dirs = jones.shape
    count = pairs.shape[1]
    groups = -(-count // GROUP)
    lanes = groups * GROUP
    rows = 8 * dirs
    unit = (3, 8, GROUP)
    planes = SIDE * SIDE
    dma = pltpu.SemaphoreType.DMA
    inverse = [[float(v) for v in row] for row in gram_inverse(channels).astype(np.float32)]
    vmem = pl.BlockSpec(memory_space=pltpu.VMEM)
    smem = pl.BlockSpec(memory_space=pltpu.SMEM)
    anywhere = pl.BlockSpec(memory_space=pl.ANY)
    return pl.pallas_call(
        functools.partial(descend_kernel, channels, blocks, inverse),
        out_shape=tuple(pltpu.VMEM(a.shape, F32) for a in (jones, duals, consensus)),
        in_specs=[anywhere, smem] + [anywhere] * 5,
        out_specs=(vmem, vmem, vmem),
        scratch_shapes=[
            pltpu.VMEM((stations // 2 + 1,) + unit, F32),
            pltpu.VMEM((8, lanes), jnp.int32),
            pltpu.VMEM((own, 8, lanes), F32),
            pltpu.VMEM((own, 8, dirs, GROUP), BF16),
            pltpu.VMEM((groups, GROUP, 4 * GROUP), BF16),
            pltpu.VMEM((own, 8, dirs, GROUP), F32),
            pltpu.VMEM((own, 8, dirs, GROUP), F32),
            pltpu.VMEM((own, stations, 8, dirs), F32),
            [pltpu.VMEM((rows, 2 * GROUP), F32)] * own,
            [pltpu.VMEM((rows, GROUP), F32)] * own,
            [pltpu.VMEM((rows, GROUP), F32)] * own,
            [pltpu.VMEM((rows, 4 * GROUP), BF16)] * own,
            [pltpu.VMEM((rows, GROUP), F32)] * own,
        ]
        + [pltpu.VMEM(a.shape, a.dtype) for a in (pairs, jones, duals, consensus, visibilities, coherencies)]
        + [dma((5 + 8 * own,))]
        + [pltpu.VMEM((planes,) + unit, F32)] * 3
        + [pltpu.VMEM((SIDE,) + unit, F32), pltpu.VMEM((2 * planes,) + unit, F32)]
        + [dma((planes,))] * 4
        + [dma((SIDE,))] * 2
        + [dma((planes,))] * 4,
        compiler_params=pltpu.CompilerParams(
            collective_id=0, has_side_effects=True, vmem_limit_bytes=56 * 2**20
        ),
        name="descend",
    )(pairs, counts, jones, duals, consensus, visibilities, coherencies)


def agree_kernel(
    channels, blocks, inverse, s_ref, jones_ref, duals_ref, consensus_out, duals_out,
    recv_core, mid, recv_plane, recv_col, full, s1, r1, s2, r2, s3, r3, s4, r4, s5, r5,
):
    z = lax.axis_index("grp"); chan = lax.axis_index("chan")
    core = chan % 2; u = chan // 2; x = u // SIDE; y = u % SIDE
    other = 1 - core
    def peer(dx, dy):
        return ((x + dx) % SIDE) * SIDE + (y + dy) % SIDE
    steps = sorted([(dx, dy) for dx in range(SIDE) for dy in range(SIDE) if dx or dy], key=lambda s: -(min(s[0],4-s[0])+min(s[1],4-s[1])))
    def back(dx, dy):
        return ((x - dx + SIDE) % SIDE) * SIDE + (y - dy + SIDE) % SIDE
    def dev(uu, cc): return {"grp": z, "chan": uu * 2 + cc}
    greet(True)
    order = steps + [(0, 0)]
    def rc(src, dst, ss, rs, d):
        return pltpu.make_async_remote_copy(src_ref=src, dst_ref=dst, send_sem=ss, recv_sem=rs, device_id=d, device_id_type=MESH)
    c1 = []
    for n, (dx, dy) in enumerate(order):
        c = rc(s_ref.at[other * 16 + peer(dx, dy)], recv_core.at[n], s1.at[n], r1.at[n], dev(u, other))
        c.start(); c1.append(c)
    c2 = []
    for n, (dx, dy) in enumerate(order):
        c1[n].wait_recv()
        mid[n] = s_ref[core * 16 + peer(dx, dy)] + recv_core[n]
        if n < 15:
            c = rc(mid.at[n], recv_plane.at[n], s2.at[n], r2.at[n], dev(peer(dx, dy), core))
            c.start(); c2.append(c)
    total = mid[15]
    for n in range(15):
        c2[n].wait_recv()
        total = total + recv_plane[n]
    recv_col[z] = total
    c3 = []
    for dz in range(1, SIDE):
        c = rc(recv_col.at[z], recv_col.at[z], s3.at[dz], r3.at[dz], {"grp": (z + dz) % SIDE, "chan": chan})
        c.start(); c3.append(c)
    for c in c3: c.wait_recv()
    total = recv_col[0] + recv_col[1] + recv_col[2] + recv_col[3]
    mine = core * 16 + u
    for i in range(3):
        full[mine, i] = sum(inverse[i][j] * total[j] for j in range(3))
    c4 = []
    for n, (dx, dy) in enumerate(steps):
        c = rc(full.at[mine], full.at[mine], s4.at[n], r4.at[n], dev(peer(dx, dy), core))
        c.start(); c4.append(c)
    c5 = []
    c = rc(full.at[mine], full.at[mine], s5.at[15], r5.at[15], dev(u, other))
    c.start(); c5.append(c)
    for n, (dx, dy) in reversed(list(enumerate(steps))):
        c4[n].wait_recv()
        unit = core * 16 + back(dx, dy)
        c = rc(full.at[unit], full.at[unit], s5.at[n], r5.at[n], dev(u, other))
        c.start(); c5.append(c)
    own, stations, _, dirs = jones_ref.shape
    near = stations // 2
    offset = (z * blocks + chan) * own
    basis = [bernstein(((offset + channel).astype(F32) + 0.5) * (1.0 / channels)) for channel in range(own)]

    def finish(unit):
        @pl.when(unit < near)
        def _():
            for side in range(2):
                station = unit + side * near
                agreed = [full[unit, i, :, side * dirs : (side + 1) * dirs] for i in range(3)]
                for i in range(3):
                    consensus_out[i, station] = agreed[i]
                for channel in range(own):
                    smooth = sum(basis[channel][i] * agreed[i] for i in range(3))
                    duals_out[channel, station] = duals_ref[channel, station] + RHO_PENALTY * (
                        jones_ref[channel, station] - smooth
                    )

    finish(mine)
    for dx, dy in reversed(steps):
        finish(core * 16 + back(dx, dy))
    for n, c in enumerate(c5):
        c.wait_recv()
        dx, dy = ([(0, 0)] + list(reversed(steps)))[n]
        finish(other * 16 + back(dx, dy))
    for c in c1 + c2 + c3 + c4 + c5: c.wait_send()


def deliver_kernel(*refs):
    half = len(refs) // 2
    copies = [pltpu.make_async_copy(refs[n], refs[half + n], refs[-1].at[n]) for n in range(half)]
    for copy in copies:
        copy.start()
    for copy in copies:
        copy.wait()


def deliver(arrays):
    return pl.pallas_call(
        deliver_kernel,
        out_shape=tuple(jax.ShapeDtypeStruct(a.shape, a.dtype) for a in arrays),
        in_specs=[pl.BlockSpec(memory_space=pltpu.VMEM)] * len(arrays),
        out_specs=tuple(pl.BlockSpec(memory_space=pl.ANY) for _ in arrays),
        scratch_shapes=[pltpu.SemaphoreType.DMA((len(arrays),))],
        compiler_params=pltpu.CompilerParams(vmem_limit_bytes=2**20),
        name="deliver",
    )(*arrays)


def shards(jones_start, duals_start, consensus_start, visibilities, coherencies, pairs, counts):
    blocks = lax.axis_size("chan")
    channels = jones_start.shape[0] * lax.axis_size("grp") * blocks
    jones, duals, consensus = (jnp.transpose(a, (0, 3, 1, 2)) for a in (jones_start, duals_start, consensus_start))
    outs = descend(channels, blocks, pairs, counts, jones, duals, consensus, visibilities, coherencies)
    return tuple(jnp.transpose(a, (0, 2, 3, 1)) for a in deliver(outs))


def solution(mesh):
    in_specs = (
        P(("grp", "chan"), None, None, None),
        P(("grp", "chan"), None, None, None),
        P(),
        P(("grp", "chan"), None, None),
        P(("grp", "chan"), None, None, None),
        P(),
        P(("grp", "chan")),
    )
    out_specs = (P(("grp", "chan"), None, None, None), P(("grp", "chan"), None, None, None), P())
    return jax.shard_map(shards, mesh=mesh, in_specs=in_specs, out_specs=out_specs, check_vma=False)
```
